32 devices in a mesh: grid: 16 (over z, y, core), orb: 2 (over x).
Axes of the slice: x: 2, y: 2, z: 4, core: 2. Of those that a mesh axis runs over, the one named last changes fastest.
Arguments:
- orbitals: bfloat16 [16, 884736], P('orb', 'grid'), may hold values from -6 to 6
- potential: float32 [884736], P('grid'), may hold values from -2 to 0
- projector_atom: int32 [24576], P('grid'), may hold values from 0 to 63, as said below
- projector_cell: int32 [24576], P('grid'), may hold values from 0 to 55295
- projector_value: float32 [24576], P('grid'), may hold values from -1.5 to 1.5
- atom_strength: float32 [64], replicated, may hold values from 0.25 to 2
- ritz_rotation: bfloat16 [4, 8, 32], P(None, None, 'orb'), may hold values from -1 to 1
- panel_owner: int32 [4], replicated, may hold values from 0 to 1
Outputs:
- filtered: bfloat16 [16, 884736], P('orb', 'grid')
- rotated: bfloat16 [32, 884736], P('orb', 'grid')
The draws below stay inside these ranges and needn't reach their ends.
Inputs may be any that keep to these rules, and one draw needn't show every extreme that they name: `projector_atom`: the entries e of slab s (e // 1536 = s) name atoms of slabs s - 1, s and s + 1 only, slab t holding atoms t * 4 to (t + 1) * 4 - 1.
All inputs are finite; a program needn't handle non-finite values.
Results may differ from the reference program's by a relative error of at most 0.0049.
Values may be sent and summed in bfloat16 or wider, within the bound.
No kernel may reach another device: no remote copies, remote signals or barrier semaphores. Data moves between devices by JAX's collectives and lax.ppermute only.
A program may use at most 128 MiB of HBM per device.

```python
import math
import jax
import jax.numpy as jnp
from jax import lax

NX = 96
NY = 96
REACH = 6
PANEL = 8
STEPS = 4
ATOM_DEV = 4
ENTRY_DEV = 1536
CELL_DEV = 55296
CELLS = 884736
NORB = 16
RITZ = 32
NATOM = 64
ENTRIES = 24576
N_ORB = 2


def draw_projector_atom(key, part):
    slab_count = NATOM // ATOM_DEV
    owner_slab = jnp.arange(ENTRIES, dtype=jnp.int32) // ENTRY_DEV
    offset_key, member_key = jax.random.split(key)
    offsets = jax.random.randint(offset_key, (ENTRIES,), -1, 2, dtype=jnp.int32)
    target = jnp.clip(owner_slab + offsets, 0, slab_count - 1)
    member = jax.random.randint(member_key, (ENTRIES,), 0, ATOM_DEV, dtype=jnp.int32)
    return (target * ATOM_DEV + member).astype(jnp.int32)


def with_ends(drawn, rng, smallest, largest):
    extent = drawn.shape
    place = [jax.random.randint(jax.random.fold_in(rng, axis), (), 0, extent[axis]) for axis in range(len(extent))]
    drawn = drawn.at[tuple(place)].set(smallest)
    longest = extent.index(max(extent))
    place[longest] = (place[longest] + 1) % extent[longest]
    return drawn.at[tuple(place)].set(largest)


def steps_of(key, extent, cuts, smallest, largest):
    def one(axis_at, parts):
        heights = jax.random.uniform(jax.random.fold_in(jax.random.fold_in(key, 6), axis_at), (parts,), jnp.float32, smallest / len(cuts), largest / len(cuts))
        return jnp.repeat(jnp.exp(heights), extent[axis_at] // parts).reshape((-1,) + (1,) * (len(extent) - axis_at - 1))

    factor_of = one(*cuts[0])
    for cut in cuts[1:]:
        factor_of = factor_of * one(*cut)
    return factor_of


def normal_values(own_key, shape, width, most, shards=(), kind=jnp.bfloat16):
    factor_of = steps_of(own_key, shape, shards, -0.22, 0.18) if shards else 1.0
    values = jax.random.normal(own_key, shape, jnp.float32) * width * factor_of
    return jnp.minimum(jnp.maximum(values, -most), most).astype(kind)


def setup_inputs(seed: int = 0) -> dict:
    streams_of = jax.random.split(jax.random.key(seed), 9)
    orbitals = normal_values(streams_of[0], (NORB, CELLS), 1.0, 6.0, ((0, 2), (1, 16)))
    potential = jnp.clip(-2.0 + 2.0 * jax.random.uniform(streams_of[1], (CELLS,), jnp.float32) ** steps_of(streams_of[1], (CELLS,), ((0, 16),), -0.2, 0.2), -2.0, 0.0)
    projector_atom = draw_projector_atom(jax.random.fold_in(streams_of[8], 71), 0)
    projector_cell = with_ends(jax.random.randint(streams_of[3], (ENTRIES,), 0, CELL_DEV), jax.random.fold_in(streams_of[3], 1), 0, CELL_DEV - 1).astype(jnp.int32)
    projector_value = normal_values(streams_of[4], (ENTRIES,), 0.25, 1.5, ((0, 16),), jnp.float32)
    atom_strength = jnp.clip(jnp.exp(jax.random.uniform(streams_of[5], (NATOM,), jnp.float32, math.log(0.25), math.log(2.0))), 0.25, 2.0)
    ritz_rotation = normal_values(streams_of[6], (STEPS, PANEL, RITZ), (STEPS * PANEL) ** -0.5, 1.0, ((2, 2),))
    panel_owner = with_ends(jax.random.randint(streams_of[7], (STEPS,), 0, N_ORB), jax.random.fold_in(streams_of[7], 1), 0, N_ORB - 1).astype(jnp.int32)
    return {"orbitals": orbitals, "potential": potential, "projector_atom": projector_atom, "projector_cell": projector_cell, "projector_value": projector_value, "atom_strength": atom_strength, "ritz_rotation": ritz_rotation, "panel_owner": panel_owner}


stencil_weights = (-5369.0 / 1800.0, 12.0 / 7.0, -15.0 / 56.0, 10.0 / 189.0, -1.0 / 112.0, 2.0 / 1925.0, -1.0 / 16632.0)
cheb_center = 6.0
cheb_half = 6.0


def laplace(extended, cell_count, column_pos, row_pos):
    plane_cells = NX * NY
    margin = REACH * plane_cells
    middle = extended[:, margin:margin + cell_count].astype(jnp.float32)
    summed = 3.0 * stencil_weights[0] * middle
    for distance in range(1, REACH + 1):
        plane_jump = distance * plane_cells
        row_jump = distance * NX
        upper_plane = extended[:, margin + plane_jump:margin + plane_jump + cell_count].astype(jnp.float32)
        lower_plane = extended[:, margin - plane_jump:margin - plane_jump + cell_count].astype(jnp.float32)
        row_after = extended[:, margin + row_jump:margin + row_jump + cell_count].astype(jnp.float32)
        row_before = extended[:, margin - row_jump:margin - row_jump + cell_count].astype(jnp.float32)
        cell_after = extended[:, margin + distance:margin + distance + cell_count].astype(jnp.float32)
        cell_before = extended[:, margin - distance:margin - distance + cell_count].astype(jnp.float32)
        neighbours = upper_plane + lower_plane
        neighbours = neighbours + jnp.where(row_pos + distance < NY, row_after, 0.0) + jnp.where(row_pos >= distance, row_before, 0.0)
        neighbours = neighbours + jnp.where(column_pos + distance < NX, cell_after, 0.0) + jnp.where(column_pos >= distance, cell_before, 0.0)
        summed = summed + stencil_weights[distance] * neighbours
    return middle, summed


def nonlocal_part(middle, cell_index, projector_atom, projector_value, atom_strength):
    gathered = jnp.take(middle, cell_index, axis=1)
    weighted = gathered * projector_value
    atom_sums = jax.ops.segment_sum(weighted.T, projector_atom, num_segments=NATOM)
    scaled = atom_sums * atom_strength[:, None]
    spread = jnp.take(scaled, projector_atom, axis=0).T * projector_value
    return jnp.zeros_like(middle).at[:, cell_index].add(spread)


def hamiltonian(field, potential, cell_index, projector_atom, projector_value, atom_strength, column_pos, row_pos):
    margin = REACH * NX * NY
    extended = jnp.pad(field, ((0, 0), (margin, margin)))
    middle, summed = laplace(extended, field.shape[1], column_pos, row_pos)
    nonlocal_term = nonlocal_part(middle, cell_index, projector_atom, projector_value, atom_strength)
    return -0.5 * summed + potential * middle + nonlocal_term


def reference(orbitals, potential, projector_atom, projector_cell, projector_value, atom_strength, ritz_rotation, panel_owner):
    cell_ids = jnp.arange(CELLS, dtype=jnp.int32)
    column_pos = cell_ids % NX
    row_pos = (cell_ids // NX) % NY
    cell_index = (jnp.arange(ENTRIES, dtype=jnp.int32) // ENTRY_DEV) * CELL_DEV + projector_cell

    def apply_field(field):
        return hamiltonian(field, potential, cell_index, projector_atom, projector_value, atom_strength, column_pos, row_pos)

    def filter_panel(panel):
        initial = panel.astype(jnp.float32)
        first_image = apply_field(panel)
        step_field = (first_image - cheb_center * initial) / cheb_half
        second = apply_field(step_field)
        return (2.0 * (second - cheb_center * step_field) / cheb_half - initial).astype(jnp.bfloat16)

    filtered = lax.map(filter_panel, orbitals.reshape(N_ORB, PANEL, CELLS)).reshape(NORB, CELLS)
    stacked = jnp.take(filtered.reshape(N_ORB, PANEL, CELLS), panel_owner, axis=0).reshape(STEPS * PANEL, CELLS)
    rotation_rows = ritz_rotation.reshape(STEPS * PANEL, RITZ)
    row_blocks = rotation_rows.T.reshape(8, RITZ // 8, STEPS * PANEL)
    rotated = lax.map(lambda block_rows: jnp.dot(block_rows, stacked, preferred_element_type=jnp.float32).astype(jnp.bfloat16), row_blocks)
    return filtered, rotated.reshape(RITZ, CELLS)
```

```python
import functools

import jax
import jax.numpy as jnp
import numpy as np
from jax import lax
from jax.experimental import pallas as pl
from jax.experimental.pallas import tpu as pltpu
from jax.sharding import PartitionSpec as P

NX = 96
NY = 96
REACH = 6
ATOM_DEV = 4
PLANE = NX * NY
BLOCK_ROWS = 8
BLOCK = BLOCK_ROWS * NX
SLOTS = 16
TILE = 256
LANES = 128

stencil_weights = (
    -5369.0 / 1800.0,
    12.0 / 7.0,
    -15.0 / 56.0,
    10.0 / 189.0,
    -1.0 / 112.0,
    2.0 / 1925.0,
    -1.0 / 16632.0,
)
cheb_center = 6.0
cheb_half = 6.0

TAPS = {
    0: ((0, 0, 3), (1, 0, 3), (2, 0, 1)),
    1: ((0, 1, 3), (1, 0, 3), (2, 0, 2)),
    2: ((0, 2, 3), (1, 0, 3), (2, 0, 3)),
}


def plane_taps():
    cell = np.arange(BLOCK)
    row, column = cell // NX, cell % NX
    out = np.zeros((3, BLOCK, BLOCK), np.float64)
    for block in range(3):
        source_row = row + (block - 1) * BLOCK_ROWS
        jump_row = np.abs(source_row[:, None] - row[None, :])
        jump_column = np.abs(column[:, None] - column[None, :])
        for distance in range(1, REACH + 1):
            hit = ((jump_row == distance) & (jump_column == 0)) | (
                (jump_row == 0) & (jump_column == distance)
            )
            out[block][hit] = stencil_weights[distance] / stencil_weights[1]
    return out.astype(jnp.bfloat16)


def z_sum(planes, target, first):
    total = None
    for at, values in enumerate(planes):
        distance = abs(first + at - target)
        if 1 <= distance <= REACH:
            term = stencil_weights[distance] * values
            total = term if total is None else total + term
    return total


def block_diagonal(depth, rows, columns):
    row = lax.broadcasted_iota(jnp.int32, (depth * rows, depth * columns), 0) // rows
    column = lax.broadcasted_iota(jnp.int32, (depth * rows, depth * columns), 1) // columns
    return row == column


def pack_planes(source, target, depth, panel, blocks, part):
    stride = depth * panel
    zero = jnp.zeros((stride, BLOCK), jnp.bfloat16)
    target[0:stride, :] = zero
    target[(blocks + 1) * stride : (blocks + 2) * stride, :] = zero

    def one(block, carry):
        for pair in range(depth // 2):
            halves = []
            for plane in (2 * pair, 2 * pair + 1):
                start = pl.multiple_of(plane * PLANE + block * BLOCK, LANES)
                halves.append(part(source[:, pl.ds(start, BLOCK)].astype(jnp.float32)))
            packed = jnp.concatenate(halves, axis=0).astype(jnp.bfloat16)
            start = pl.multiple_of((block + 1) * stride + pair * 2 * panel, 16)
            target[pl.ds(start, 2 * panel), :] = packed
        return carry

    lax.fori_loop(0, blocks, one, 0)


def apply_taps(packs, taps, out, stride, blocks):
    rows = blocks * stride
    for tile, parts in TAPS.items():
        total = None
        for packed in packs:
            for block, low, high in parts:
                term = jnp.dot(
                    packed[block * stride : block * stride + rows, low * TILE : high * TILE],
                    taps[block, low * TILE : high * TILE, tile * TILE : (tile + 1) * TILE],
                    preferred_element_type=jnp.float32,
                )
                total = term if total is None else total + term
        out[:, tile * TILE : (tile + 1) * TILE] = total


def atom_partial(packs, table, out, depth, panel, blocks):
    stride, atoms = depth * panel, depth * SLOTS

    def one(block, total):
        weights = table[pl.ds(pl.multiple_of(block * atoms, 16), atoms), :]
        for packed in packs:
            rows = packed[pl.ds(pl.multiple_of((block + 1) * stride, 16), stride), :]
            total = total + lax.dot_general(
                rows, weights, (((1,), (1,)), ((), ())), preferred_element_type=jnp.float32
            )
        return total

    total = lax.fori_loop(0, blocks, one, jnp.zeros((stride, atoms), jnp.float32))
    total = jnp.where(block_diagonal(depth, panel, SLOTS), total, 0.0)
    folded = total[0:panel, :]
    for plane in range(1, depth):
        folded = folded + total[plane * panel : (plane + 1) * panel, :]
    slot = lax.broadcasted_iota(jnp.int32, (atoms, LANES), 0) % SLOTS
    lane = lax.broadcasted_iota(jnp.int32, (atoms, LANES), 1)
    out[...] = jnp.dot(
        folded,
        (slot == lane).astype(jnp.float32),
        precision=lax.Precision.HIGHEST,
        preferred_element_type=jnp.float32,
    )


def spread_rows(tables, strength, depth, panel):
    total = None
    for offset, table in tables.items():
        value = table[...]
        if offset:
            value = pltpu.roll(value, (offset * ATOM_DEV) % LANES, 1)
        total = value if total is None else total + value
    lane = lax.broadcasted_iota(jnp.int32, total.shape, 1)
    total = jnp.where(lane < 3 * ATOM_DEV, total * strength[...], 0.0)
    slot = lax.broadcasted_iota(jnp.int32, (LANES, depth * SLOTS), 1) % SLOTS
    lane = lax.broadcasted_iota(jnp.int32, (LANES, depth * SLOTS), 0)
    wide = jnp.dot(
        total,
        (slot == lane).astype(jnp.float32),
        precision=lax.Precision.HIGHEST,
        preferred_element_type=jnp.float32,
    )
    wide = jnp.where(
        block_diagonal(depth, panel, SLOTS), jnp.concatenate([wide] * depth, axis=0), 0.0
    )
    high = wide.astype(jnp.bfloat16)
    return high, (wide - high.astype(jnp.float32)).astype(jnp.bfloat16)


def local_part(field, potential, sums, out, depth, panel, blocks, finish):
    def one(block, carry):
        for part in range(BLOCK // TILE):
            starts = [
                pl.multiple_of(plane * PLANE + block * BLOCK + part * TILE, LANES)
                for plane in range(depth)
            ]
            planes = [field[:, pl.ds(start, TILE)].astype(jnp.float32) for start in starts]
            for plane in range(depth):
                row = pl.multiple_of(block * depth * panel + plane * panel, 8)
                lap = (
                    3.0 * stencil_weights[0] * planes[plane]
                    + stencil_weights[1]
                    * sums[pl.ds(row, panel), part * TILE : (part + 1) * TILE]
                    + z_sum(planes, plane, 0)
                )
                first = plane * (PLANE // LANES) + block * (BLOCK // LANES) + part * 2
                level = jnp.concatenate(
                    [
                        jnp.broadcast_to(potential[pl.ds(first + k, 1), :], (panel, LANES))
                        for k in range(TILE // LANES)
                    ],
                    axis=1,
                )
                cells = pl.ds(starts[plane], TILE)
                out[:, cells] = finish(planes[plane], lap, level, cells)
        return carry

    lax.fori_loop(0, blocks, one, 0)


def halo_part(low, high, rows, table, emit, depth, panel, blocks):
    atoms = depth * SLOTS
    stride = depth * panel
    row_high, row_low = rows

    def one(block, carry):
        weights = table[pl.ds(pl.multiple_of(block * atoms, 16), atoms), :]
        spread = jnp.dot(row_high, weights, preferred_element_type=jnp.float32)
        spread = spread + jnp.dot(row_low, weights, preferred_element_type=jnp.float32)
        for part in range(BLOCK // TILE):
            cut = slice(part * TILE, (part + 1) * TILE)
            starts = [
                pl.multiple_of(plane * PLANE + block * BLOCK + part * TILE, LANES)
                for plane in range(depth)
            ]
            below = [low[:, pl.ds(start, TILE)].astype(jnp.float32) for start in starts]
            sums = [z_sum(below, plane, -depth) for plane in range(depth)]
            above = [high[:, pl.ds(start, TILE)].astype(jnp.float32) for start in starts]
            for plane in range(depth):
                lap = sums[plane] + z_sum(above, plane, depth)
                near = spread[plane * panel : (plane + 1) * panel, cut]
                emit(pl.ds(starts[plane], TILE), lap, near)
        return carry

    lax.fori_loop(0, blocks, one, 0)


def first_local_kernel(
    depth, panel, blocks, field, potential, row_ref, lane_ref, value_ref, taps,
    table, partial, out, packed, sums, place,
):
    stride, atoms = depth * panel, depth * SLOTS
    entries = row_ref.shape[1]
    lane = lax.broadcasted_iota(jnp.int32, (BLOCK, entries), 0)
    place[...] = jnp.where(lane == lane_ref[...], value_ref[...], 0.0).astype(jnp.bfloat16)
    chunk = 4 * atoms

    def build(at, carry):
        first = pl.multiple_of(at * chunk, 16)
        row = lax.broadcasted_iota(jnp.int32, (chunk, entries), 0) + first
        hit = jnp.where(row == row_ref[...], 1.0, 0.0).astype(jnp.bfloat16)
        table[pl.ds(first, chunk), :] = lax.dot_general(
            hit, place[...], (((1,), (1,)), ((), ())), preferred_element_type=jnp.float32
        ).astype(jnp.bfloat16)
        return carry

    lax.fori_loop(0, blocks * atoms // chunk, build, 0)
    pack_planes(field, packed, depth, panel, blocks, lambda x: x)
    atom_partial((packed,), table, partial, depth, panel, blocks)
    apply_taps((packed,), taps, sums, stride, blocks)

    def finish(values, lap, level, cells):
        return (-0.5 * lap + (level - cheb_center) * values) * (1.0 / cheb_half)

    local_part(field, potential, sums, out, depth, panel, blocks, finish)


def first_halo_kernel(
    depth, panel, blocks, local, low, high, table, strength, *refs
):
    *tables, out, sent = refs
    tables = dict(zip((0, 1, -1, 2, -2), tables))
    rows = spread_rows(tables, strength, depth, panel)

    def emit(cells, lap, near):
        value = local[:, cells] + (near - 0.5 * lap) * (1.0 / cheb_half)
        out[:, cells] = value
        sent[:, cells] = value.astype(jnp.bfloat16)

    halo_part(low, high, rows, table, emit, depth, panel, blocks)


def second_local_kernel(
    depth, panel, blocks, field, initial, potential, table, taps,
    partial, out, packed, rest, sums,
):
    stride = depth * panel
    pack_planes(field, packed, depth, panel, blocks, lambda x: x)
    pack_planes(
        field, rest, depth, panel, blocks,
        lambda x: x - x.astype(jnp.bfloat16).astype(jnp.float32),
    )
    packs = (packed, rest)
    atom_partial(packs, table, partial, depth, panel, blocks)
    apply_taps(packs, taps, sums, stride, blocks)

    def finish(values, lap, level, cells):
        return (-0.5 * lap + (level - cheb_center) * values) * (2.0 / cheb_half) - initial[
            :, cells
        ].astype(jnp.float32)

    local_part(field, potential, sums, out, depth, panel, blocks, finish)


def second_halo_kernel(depth, panel, blocks, local, low, high, table, strength, *refs):
    *tables, out = refs
    tables = dict(zip((0, 1, -1, 2, -2), tables))
    rows = spread_rows(tables, strength, depth, panel)

    def emit(cells, lap, near):
        value = local[:, cells] + (near - 0.5 * lap) * (2.0 / cheb_half)
        out[:, cells] = value.astype(jnp.bfloat16)

    halo_part(low, high, rows, table, emit, depth, panel, blocks)


def rotate_kernel(rotation_high, rotation_low, *refs):
    *panels, out = refs
    rows = jnp.concatenate([p[...].astype(jnp.float32) for p in panels], axis=0).astype(
        jnp.bfloat16
    )
    total = jnp.dot(rotation_high[...], rows, preferred_element_type=jnp.float32)
    total = total + jnp.dot(rotation_low[...], rows, preferred_element_type=jnp.float32)
    out[...] = total.astype(jnp.bfloat16)


def call(kernel, out_shape, scratch, flops, *operands):
    bytes_accessed = sum(int(np.prod(o.shape)) * o.dtype.itemsize for o in operands)
    return pl.pallas_call(
        kernel,
        out_shape=out_shape,
        in_specs=[pl.BlockSpec(memory_space=pltpu.VMEM)] * len(operands),
        out_specs=jax.tree.map(lambda _: pl.BlockSpec(memory_space=pltpu.VMEM), out_shape),
        scratch_shapes=scratch,
        compiler_params=pltpu.CompilerParams(vmem_limit_bytes=48 * 2**20),
        cost_estimate=pl.CostEstimate(
            flops=flops, bytes_accessed=bytes_accessed, transcendentals=0
        ),
    )(*operands)


def shifted(block, offset):
    count = lax.axis_size("grid")
    pairs = [(i, i + offset) for i in range(count) if 0 <= i + offset < count]
    return lax.ppermute(block, "grid", pairs)


def body(
    orbitals,
    potential,
    projector_atom,
    projector_cell,
    projector_value,
    atom_strength,
    ritz_rotation,
    panel_owner,
):
    panel, cells = orbitals.shape
    depth = cells // PLANE
    blocks = PLANE // BLOCK
    stride, atoms = depth * panel, depth * SLOTS
    entries = projector_atom.shape[0]
    slab_index = lax.axis_index("grid")
    taps = jnp.asarray(plane_taps())
    level = potential.reshape(cells // LANES, LANES)

    plane = projector_cell // PLANE
    inside = projector_cell % PLANE
    slot = projector_atom - (slab_index - 1) * ATOM_DEV
    row_at = ((inside // BLOCK) * depth + plane) * SLOTS + slot
    lane_at = inside % BLOCK
    padded_strength = jnp.pad(atom_strength, (ATOM_DEV, LANES))
    strength = lax.dynamic_slice_in_dim(padded_strength, slab_index * ATOM_DEV, LANES)[None, :]

    bf16, f32 = jnp.bfloat16, jnp.float32
    shape = jax.ShapeDtypeStruct
    field = shape((panel, cells), f32)
    narrow = shape((panel, cells), bf16)
    sums = shape((panel, LANES), f32)
    packed = pltpu.VMEM(((blocks + 2) * stride, BLOCK), bf16)
    tap_sums = pltpu.VMEM((blocks * stride, BLOCK), f32)
    sizes = (depth, panel, blocks)

    below, above = shifted(orbitals, 1), shifted(orbitals, -1)
    table, partial, local = call(
        functools.partial(first_local_kernel, *sizes),
        (shape((blocks * atoms, BLOCK), bf16), sums, field),
        [packed, tap_sums, pltpu.VMEM((BLOCK, entries), bf16)],
        5 * 10**9,
        orbitals, level, row_at[None, :], lane_at[None, :], projector_value[None, :], taps,
    )
    near = [partial] + [shifted(partial, -k) for k in (1, -1, 2, -2)]
    step_field, sent = call(
        functools.partial(first_halo_kernel, *sizes),
        (field, narrow), [], 10**9,
        local, below, above, table, strength, *near,
    )
    below, above = shifted(sent, 1), shifted(sent, -1)
    partial, local = call(
        functools.partial(second_local_kernel, *sizes),
        (sums, field), [packed, packed, tap_sums], 4 * 10**9,
        step_field, orbitals, level, table, taps,
    )
    near = [partial] + [shifted(partial, -k) for k in (1, -1, 2, -2)]
    filtered = call(
        functools.partial(second_halo_kernel, *sizes),
        narrow, [], 10**9,
        local, below, above, table, strength, *near,
    )

    orb_count = lax.axis_size("orb")
    orb_index = lax.axis_index("orb")
    panels = [filtered]
    for k in range(1, orb_count):
        panels.append(
            lax.ppermute(filtered, "orb", [(i, (i + k) % orb_count) for i in range(orb_count)])
        )
    source = (orb_index - jnp.arange(orb_count)) % orb_count
    chosen = (panel_owner[None, :] == source[:, None]).astype(f32)
    rotation = jnp.sum(
        chosen[:, :, None, None] * ritz_rotation.astype(f32)[None], axis=1
    )
    rotation = rotation.reshape(orb_count * panel, ritz_rotation.shape[2]).T
    rotation_high = rotation.astype(bf16)
    rotation_low = (rotation - rotation_high.astype(f32)).astype(bf16)
    columns = ritz_rotation.shape[2]
    rotated = pl.pallas_call(
        rotate_kernel,
        grid=(depth,),
        out_shape=shape((columns, cells), bf16),
        in_specs=[pl.BlockSpec(rotation.shape, lambda i: (0, 0))] * 2
        + [pl.BlockSpec((panel, PLANE), lambda i: (0, i))] * orb_count,
        out_specs=pl.BlockSpec((columns, PLANE), lambda i: (0, i)),
        compiler_params=pltpu.CompilerParams(vmem_limit_bytes=48 * 2**20),
    )(rotation_high, rotation_low, *panels)
    return (filtered, rotated)


def solution(mesh):
    in_specs = (
        P("orb", "grid"),
        P("grid"),
        P("grid"),
        P("grid"),
        P("grid"),
        P(),
        P(None, None, "orb"),
        P(),
    )
    out_specs = (P("orb", "grid"), P("orb", "grid"))
    return jax.shard_map(body, mesh=mesh, in_specs=in_specs, out_specs=out_specs, check_vma=False)
```

```python
import functools

import jax
import jax.numpy as jnp
import numpy as np
from jax import lax
from jax.experimental import pallas as pl
from jax.experimental.pallas import tpu as pltpu
from jax.sharding import PartitionSpec as P

NX = 96
NY = 96
REACH = 6
ATOM_DEV = 4
PLANE = NX * NY
BLOCK_ROWS = 8
BLOCK = BLOCK_ROWS * NX
SLOTS = 16
TILE = 256
LANES = 128
VMEM_LIMIT = 24 * 2**20

stencil_weights = (
    -5369.0 / 1800.0,
    12.0 / 7.0,
    -15.0 / 56.0,
    10.0 / 189.0,
    -1.0 / 112.0,
    2.0 / 1925.0,
    -1.0 / 16632.0,
)
cheb_center = 6.0
cheb_half = 6.0

TAPS = {
    0: ((0, 0, 3), (1, 0, 3), (2, 0, 1)),
    1: ((0, 1, 3), (1, 0, 3), (2, 0, 2)),
    2: ((0, 2, 3), (1, 0, 3), (2, 0, 3)),
}


def plane_taps():
    cell = np.arange(BLOCK)
    row, column = cell // NX, cell % NX
    out = np.zeros((3, BLOCK, BLOCK), np.float64)
    for block in range(3):
        source_row = row + (block - 1) * BLOCK_ROWS
        jump_row = np.abs(source_row[:, None] - row[None, :])
        jump_column = np.abs(column[:, None] - column[None, :])
        for distance in range(1, REACH + 1):
            hit = ((jump_row == distance) & (jump_column == 0)) | (
                (jump_row == 0) & (jump_column == distance)
            )
            out[block][hit] = stencil_weights[distance] / stencil_weights[1]
    return out.astype(jnp.bfloat16)


def z_sum(planes, target, first):
    total = None
    for at, values in enumerate(planes):
        distance = abs(first + at - target)
        if 1 <= distance <= REACH:
            term = stencil_weights[distance] * values
            total = term if total is None else total + term
    return total


def block_diagonal(depth, rows, columns):
    row = lax.broadcasted_iota(jnp.int32, (depth * rows, depth * columns), 0) // rows
    column = lax.broadcasted_iota(jnp.int32, (depth * rows, depth * columns), 1) // columns
    return row == column


def split(values):
    high = values.astype(jnp.bfloat16)
    return high, (values - high.astype(jnp.float32)).astype(jnp.bfloat16)


def aligned(index, multiple):
    return pl.multiple_of(index, multiple)


class Sizes:
    def __init__(self, panel, cells, entries):
        self.panel, self.cells, self.entries = panel, cells, entries
        self.depth = cells // PLANE
        self.blocks = PLANE // BLOCK
        self.stride = self.depth * panel
        self.atoms = self.depth * SLOTS
        self.half = panel // 2
        self.half_plane = PLANE // 2
        self.half_blocks = self.blocks // 2


def pack_planes(n, source, targets):
    zero = jnp.zeros((n.stride, BLOCK), jnp.bfloat16)
    for target in targets:
        target[0 : n.stride, :] = zero
        target[(n.blocks + 1) * n.stride : (n.blocks + 2) * n.stride, :] = zero

    def one(block, carry):
        for pair in range(n.depth // 2):
            halves = []
            for plane in (2 * pair, 2 * pair + 1):
                start = aligned(plane * PLANE + block * BLOCK, LANES)
                halves.append(source[:, pl.ds(start, BLOCK)].astype(jnp.float32))
            parts = split(jnp.concatenate(halves, axis=0))
            start = aligned((block + 1) * n.stride + pair * 2 * n.panel, 16)
            for target, part in zip(targets, parts):
                target[pl.ds(start, 2 * n.panel), :] = part
        return carry

    lax.fori_loop(0, n.blocks, one, 0)


def apply_taps(n, packs, taps, out):
    rows = n.blocks * n.stride
    for tile, parts in TAPS.items():
        total = None
        for packed in packs:
            for block, low, high in parts:
                term = jnp.dot(
                    packed[block * n.stride : block * n.stride + rows, low * TILE : high * TILE],
                    taps[block, low * TILE : high * TILE, tile * TILE : (tile + 1) * TILE],
                    preferred_element_type=jnp.float32,
                )
                total = term if total is None else total + term
        out[:, tile * TILE : (tile + 1) * TILE] = total


def atom_partial(n, packs, table, out):
    total = None
    for block in range(n.blocks):
        weights = table[block * n.atoms : (block + 1) * n.atoms, :]
        for packed in packs:
            rows = packed[(block + 1) * n.stride : (block + 2) * n.stride, :]
            term = lax.dot_general(
                rows, weights, (((1,), (1,)), ((), ())), preferred_element_type=jnp.float32
            )
            total = term if total is None else total + term
    total = jnp.where(block_diagonal(n.depth, n.panel, SLOTS), total, 0.0)
    folded = total[0 : n.panel, :]
    for plane in range(1, n.depth):
        folded = folded + total[plane * n.panel : (plane + 1) * n.panel, :]
    slot = lax.broadcasted_iota(jnp.int32, (n.atoms, LANES), 0) % SLOTS
    lane = lax.broadcasted_iota(jnp.int32, (n.atoms, LANES), 1)
    out[...] = jnp.dot(
        folded,
        (slot == lane).astype(jnp.float32),
        precision=lax.Precision.HIGHEST,
        preferred_element_type=jnp.float32,
    )


def near_sums(n, tables, strength):
    own, partner, far, partner_far = tables
    outward = 2 * (lax.axis_index("grid") % 2) - 1
    slab = lax.axis_index("grid")
    total = own[...]
    for table, offset in (
        (partner[...], -outward),
        (far[0 : n.panel, :], outward),
        (far[n.panel : 2 * n.panel, :], 2 * outward),
        (partner_far[0 : n.panel, :], -2 * outward),
        (partner_far[n.panel : 2 * n.panel, :], -3 * outward),
    ):
        total = total + pltpu.roll(table, (offset * ATOM_DEV + LANES) % LANES, 1)
    count = strength.shape[1]
    atom = lax.broadcasted_iota(jnp.int32, (count, LANES), 0)
    slot = lax.broadcasted_iota(jnp.int32, (count, LANES), 1) + (slab - 1) * ATOM_DEV
    near = jnp.dot(
        jnp.broadcast_to(strength[...], (n.panel, count)),
        (atom == slot).astype(jnp.float32),
        precision=lax.Precision.HIGHEST,
        preferred_element_type=jnp.float32,
    )
    lane = lax.broadcasted_iota(jnp.int32, total.shape, 1)
    total = jnp.where(lane < 3 * ATOM_DEV, total * near, 0.0)
    slot = lax.broadcasted_iota(jnp.int32, (LANES, n.atoms), 1) % SLOTS
    lane = lax.broadcasted_iota(jnp.int32, (LANES, n.atoms), 0)
    return jnp.dot(
        total,
        (slot == lane).astype(jnp.float32),
        precision=lax.Precision.HIGHEST,
        preferred_element_type=jnp.float32,
    )


def spread_of(n, rows, weights):
    both = jnp.dot(rows, weights, preferred_element_type=jnp.float32)
    return both[0 : n.stride, :] + both[n.stride : 2 * n.stride, :]


def halves_of(n, values):
    low, high = values
    return [
        jnp.concatenate([low[c : c + n.half, :], high[c : c + n.half, :]], axis=0)
        for c in (0, n.half)
    ]


def by_side(inner, outer, run):
    odd = lax.axis_index("grid") % 2
    pl.when(odd == 0)(functools.partial(run, outer, inner))
    pl.when(odd == 1)(functools.partial(run, inner, outer))


def tile_loop(n, one_tile):
    def one(block, carry):
        for part in range(BLOCK // TILE):
            one_tile(block, part)
        return carry

    lax.fori_loop(0, n.half_blocks, one, 0)


def level_of(n, potential, plane, block, part):
    first = plane * (PLANE // LANES) + block * (BLOCK // LANES) + part * (TILE // LANES)
    return jnp.concatenate(
        [
            jnp.broadcast_to(potential[pl.ds(first + k, 1), :], (n.panel, LANES))
            for k in range(TILE // LANES)
        ],
        axis=1,
    )


def local_lap(n, planes, plane, sums, block, part):
    row = aligned(block * n.stride + plane * n.panel, 8)
    return (
        3.0 * stencil_weights[0] * planes[plane]
        + stencil_weights[1] * sums[pl.ds(row, n.panel), part * TILE : (part + 1) * TILE]
        + z_sum(planes, plane, 0)
    )


def table_kernel(n, field, atom_ref, cell_ref, value_ref, table, partial, packed, place):
    def entry_row(ref):
        return jnp.concatenate([ref[k : k + 1, :] for k in range(n.entries // LANES)], axis=1)

    cell = entry_row(cell_ref)
    slot = entry_row(atom_ref) - (lax.axis_index("grid") - 1) * ATOM_DEV
    plane, inside = cell // PLANE, cell % PLANE
    row_at = ((inside // BLOCK) * n.depth + plane) * SLOTS + slot
    lane_at = inside % BLOCK
    lane = lax.broadcasted_iota(jnp.int32, (BLOCK, n.entries), 0)
    place[...] = jnp.where(lane == lane_at, entry_row(value_ref), 0.0).astype(jnp.bfloat16)
    chunk = 4 * n.atoms

    def build(at, carry):
        first = aligned(at * chunk, 16)
        row = lax.broadcasted_iota(jnp.int32, (chunk, n.entries), 0) + first
        hit = jnp.where(row == row_at, 1.0, 0.0).astype(jnp.bfloat16)
        table[pl.ds(first, chunk), :] = lax.dot_general(
            hit, place[...], (((1,), (1,)), ((), ())), preferred_element_type=jnp.float32
        ).astype(jnp.bfloat16)
        return carry

    lax.fori_loop(0, n.blocks * n.atoms // chunk, build, 0)
    pack_planes(n, field, (packed,))
    atom_partial(n, (packed,), table, partial)


def first_local_kernel(n, field, packed, potential, taps, out, sums):
    apply_taps(n, (packed,), taps, sums)

    def one_tile(half_block, part):
        for block in (half_block, half_block + n.half_blocks):
            starts = [
                aligned(plane * PLANE + block * BLOCK + part * TILE, LANES)
                for plane in range(n.depth)
            ]
            planes = [field[:, pl.ds(start, TILE)].astype(jnp.float32) for start in starts]
            for plane in range(n.depth):
                lap = local_lap(n, planes, plane, sums, block, part)
                level = level_of(n, potential, plane, block, part)
                out[:, pl.ds(starts[plane], TILE)] = (
                    -0.5 * lap + (level - cheb_center) * planes[plane]
                ) * (1.0 / cheb_half)

    tile_loop(n, one_tile)


def first_halo_kernel(n, local, inner, outer, table, strength, *refs):
    *tables, out, sent_first, sent_second = refs
    wide = near_sums(n, tables, strength)
    rows = jnp.where(
        block_diagonal(n.depth, n.panel, SLOTS), jnp.concatenate([wide] * n.depth, axis=0), 0.0
    )
    rows = jnp.concatenate(split(rows), axis=0)

    def one(low, high, half_block, carry):
        blocks = (half_block, half_block + n.half_blocks)
        spreads = [
            spread_of(n, rows, table[pl.ds(aligned(b * n.atoms, 16), n.atoms), :]) for b in blocks
        ]
        for part in range(BLOCK // TILE):
            cut = slice(part * TILE, (part + 1) * TILE)
            values = [[], []]
            for side, block in enumerate(blocks):
                starts = [
                    aligned(plane * PLANE + block * BLOCK + part * TILE, LANES)
                    for plane in range(n.depth)
                ]
                below = [low[:, pl.ds(start, TILE)].astype(jnp.float32) for start in starts]
                above = [high[:, pl.ds(start, TILE)].astype(jnp.float32) for start in starts]
                for plane in range(n.depth):
                    lap = z_sum(below, plane, -n.depth) + z_sum(above, plane, n.depth)
                    near = spreads[side][plane * n.panel : (plane + 1) * n.panel, cut]
                    cells = pl.ds(starts[plane], TILE)
                    value = local[:, cells] + (near - 0.5 * lap) * (1.0 / cheb_half)
                    out[:, cells] = value
                    values[side].append(value)
            for plane in range(n.depth):
                start = aligned(plane * n.half_plane + half_block * BLOCK + part * TILE, LANES)
                first, second = halves_of(n, (values[0][plane], values[1][plane]))
                sent_first[:, pl.ds(start, TILE)] = first.astype(jnp.bfloat16)
                sent_second[:, pl.ds(start, TILE)] = second.astype(jnp.bfloat16)
        return carry

    by_side(
        inner,
        outer,
        lambda low, high: lax.fori_loop(
            0, n.half_blocks, functools.partial(one, low, high), None
        ),
    )


def second_sums_kernel(n, field, table, partial, packed, rest):
    pack_planes(n, field, (packed, rest))
    atom_partial(n, (packed, rest), table, partial)


def second_local_kernel(
    n, field, packed, rest, initial, potential, taps, out_first, out_second, sums
):
    apply_taps(n, (packed, rest), taps, sums)

    def one_tile(half_block, part):
        values = [[], []]
        for side, block in enumerate((half_block, half_block + n.half_blocks)):
            starts = [
                aligned(plane * PLANE + block * BLOCK + part * TILE, LANES)
                for plane in range(n.depth)
            ]
            planes = [field[:, pl.ds(start, TILE)] for start in starts]
            for plane in range(n.depth):
                lap = local_lap(n, planes, plane, sums, block, part)
                level = level_of(n, potential, plane, block, part)
                start = initial[:, pl.ds(starts[plane], TILE)].astype(jnp.float32)
                values[side].append(
                    (-0.5 * lap + (level - cheb_center) * planes[plane]) * (2.0 / cheb_half)
                    - start
                )
        for plane in range(n.depth):
            start = aligned(plane * n.half_plane + half_block * BLOCK + part * TILE, LANES)
            first, second = halves_of(n, (values[0][plane], values[1][plane]))
            out_first[:, pl.ds(start, TILE)] = first
            out_second[:, pl.ds(start, TILE)] = second

    tile_loop(n, one_tile)


def second_halo_kernel(n, chunk, local, inner, outer, table, strength, *refs):
    *tables, out = refs
    wide = near_sums(n, tables, strength)[chunk * n.half : (chunk + 1) * n.half, :]
    rows = jnp.concatenate([wide] * (2 * n.depth), axis=0)
    rows = jnp.where(block_diagonal(n.depth, n.panel, SLOTS), rows, 0.0)
    side = lax.broadcasted_iota(jnp.int32, rows.shape, 0) // n.half % 2
    rows = [jnp.concatenate(split(jnp.where(side == at, rows, 0.0)), axis=0) for at in (0, 1)]

    def one(low, high, half_block, carry):
        spread = None
        for at, block in enumerate((half_block, half_block + n.half_blocks)):
            weights = table[pl.ds(aligned(block * n.atoms, 16), n.atoms), :]
            term = spread_of(n, rows[at], weights)
            spread = term if spread is None else spread + term
        for part in range(BLOCK // TILE):
            cut = slice(part * TILE, (part + 1) * TILE)
            starts = [
                aligned(plane * n.half_plane + half_block * BLOCK + part * TILE, LANES)
                for plane in range(n.depth)
            ]
            below = [low[:, pl.ds(start, TILE)].astype(jnp.float32) for start in starts]
            above = [high[:, pl.ds(start, TILE)].astype(jnp.float32) for start in starts]
            for plane in range(n.depth):
                lap = z_sum(below, plane, -n.depth) + z_sum(above, plane, n.depth)
                near = spread[plane * n.panel : (plane + 1) * n.panel, cut]
                cells = pl.ds(starts[plane], TILE)
                value = local[:, cells] + (near - 0.5 * lap) * (2.0 / cheb_half)
                out[:, cells] = value.astype(jnp.bfloat16)
        return carry

    by_side(
        inner,
        outer,
        lambda low, high: lax.fori_loop(
            0, n.half_blocks, functools.partial(one, low, high), None
        ),
    )


def rotate_kernel(n, columns, rotation, *refs):
    *panels, filtered, rotated = refs
    for block in range(n.half_blocks):
        cut = slice(block * BLOCK, (block + 1) * BLOCK)
        parts = [panel[:, cut].astype(jnp.float32) for panel in panels]
        stack = jnp.concatenate(parts, axis=0).astype(jnp.bfloat16)
        both = jnp.dot(rotation[...], stack, preferred_element_type=jnp.float32)
        total = both[0 : 2 * columns, :] + both[2 * columns : 4 * columns, :]
        for side in range(2):
            first = side * n.half_plane + block * BLOCK
            rows = slice(side * n.half, (side + 1) * n.half)
            filtered[:, first : first + BLOCK] = jnp.concatenate(
                [parts[0][rows, :], parts[1][rows, :]], axis=0
            ).astype(jnp.bfloat16)
            rotated[:, first : first + BLOCK] = total[
                side * columns : (side + 1) * columns, :
            ].astype(jnp.bfloat16)


def call(kernel, out_shape, scratch, flops, *operands):
    bytes_accessed = sum(int(np.prod(o.shape)) * o.dtype.itemsize for o in operands)
    return pl.pallas_call(
        kernel,
        out_shape=out_shape,
        in_specs=[pl.BlockSpec(memory_space=pltpu.VMEM)] * len(operands),
        out_specs=jax.tree.map(lambda _: pl.BlockSpec(memory_space=pltpu.VMEM), out_shape),
        scratch_shapes=scratch,
        compiler_params=pltpu.CompilerParams(vmem_limit_bytes=VMEM_LIMIT),
        cost_estimate=pl.CostEstimate(
            flops=flops, bytes_accessed=bytes_accessed, transcendentals=0
        ),
    )(*operands)


def swapped(block, partner):
    count = lax.axis_size("grid")
    pairs = [(i, partner(i)) for i in range(count) if 0 <= partner(i) < count]
    return lax.ppermute(block, "grid", pairs)


def core_partner(i):
    return i ^ 1


def outer_partner(i):
    return i + 1 if i % 2 else i - 1


def exchange_sums(partial):
    partner = swapped(partial, core_partner)
    both = jnp.concatenate([partial, partner], axis=0)
    far = swapped(both, outer_partner)
    return partial, partner, far, swapped(far, core_partner)


def body(
    orbitals,
    potential,
    projector_atom,
    projector_cell,
    projector_value,
    atom_strength,
    ritz_rotation,
    panel_owner,
):
    n = Sizes(orbitals.shape[0], orbitals.shape[1], projector_atom.shape[0])
    taps = jnp.asarray(plane_taps())
    level = potential.reshape(n.cells // LANES, LANES)
    lists = [
        entry.reshape(n.entries // LANES, LANES)
        for entry in (projector_atom, projector_cell, projector_value)
    ]
    strength = atom_strength[None, :]

    bf16, f32 = jnp.bfloat16, jnp.float32
    shape = jax.ShapeDtypeStruct
    field = shape((n.panel, n.cells), f32)
    chunk_field = shape((n.panel, n.cells // 2), f32)
    chunk_narrow = shape((n.panel, n.cells // 2), bf16)
    sums = shape((n.panel, LANES), f32)
    packed_shape = shape(((n.blocks + 2) * n.stride, BLOCK), bf16)
    tap_sums = pltpu.VMEM((n.blocks * n.stride, BLOCK), f32)

    inner = swapped(orbitals, core_partner)
    outer = swapped(orbitals, outer_partner)
    table, partial, packed = call(
        functools.partial(table_kernel, n),
        (shape((n.blocks * n.atoms, BLOCK), bf16), sums, packed_shape),
        [pltpu.VMEM((BLOCK, n.entries), bf16)],
        4 * 10**9,
        orbitals, *lists,
    )
    near = exchange_sums(partial)
    local = call(
        functools.partial(first_local_kernel, n), field, [tap_sums], 2 * 10**9,
        orbitals, packed, level, taps,
    )
    step_field, sent_first, sent_second = call(
        functools.partial(first_halo_kernel, n),
        (field, chunk_narrow, chunk_narrow), [], 10**9,
        local, inner, outer, table, strength, *near,
    )
    outers = [swapped(sent_first, outer_partner)]
    inners = [swapped(sent_first, core_partner)]
    partial, packed, rest = call(
        functools.partial(second_sums_kernel, n),
        (sums, packed_shape, packed_shape), [], 10**9,
        step_field, table,
    )
    near = exchange_sums(partial)
    sent_second, _ = lax.optimization_barrier((sent_second, near[2]))
    outers.append(swapped(sent_second, outer_partner))
    inners.append(swapped(sent_second, core_partner))
    locals_ = call(
        functools.partial(second_local_kernel, n),
        (chunk_field, chunk_field), [tap_sums], 3 * 10**9,
        step_field, packed, rest, orbitals, level, taps,
    )

    orb_count = lax.axis_size("orb")
    orb_index = lax.axis_index("orb")
    shares = []
    for chunk in range(2):
        share = call(
            functools.partial(second_halo_kernel, n, chunk),
            chunk_narrow, [], 10**8,
            locals_[chunk], inners[chunk], outers[chunk], table, strength, *near,
        )
        shares.append(
            [share]
            + [
                lax.ppermute(share, "orb", [(i, (i + k) % orb_count) for i in range(orb_count)])
                for k in range(1, orb_count)
            ]
        )
    panels = [shares[chunk][k] for k in range(orb_count) for chunk in range(2)]
    source = (orb_index - jnp.arange(orb_count)) % orb_count
    chosen = (panel_owner[None, :] == source[:, None]).astype(f32)
    rotation = jnp.sum(
        chosen[:, :, None, None] * ritz_rotation.astype(f32)[None], axis=1
    )
    columns = ritz_rotation.shape[2]
    rotation = rotation.reshape(orb_count * 2, 1, n.half, columns)
    sides = jnp.eye(2, dtype=f32)
    rotation = (
        sides[:, None, None, :, None] * rotation.transpose(3, 0, 1, 2)[None]
    ).reshape(2 * columns, orb_count * 2 * n.panel)
    rotation = jnp.concatenate(split(rotation), axis=0)
    filtered, rotated = pl.pallas_call(
        functools.partial(rotate_kernel, n, columns),
        grid=(n.depth,),
        out_shape=(shape((n.panel, n.cells), bf16), shape((columns, n.cells), bf16)),
        in_specs=[pl.BlockSpec(rotation.shape, lambda i: (0, 0))]
        + [pl.BlockSpec((n.panel, n.half_plane), lambda i: (0, i))] * len(panels),
        out_specs=(
            pl.BlockSpec((n.panel, PLANE), lambda i: (0, i)),
            pl.BlockSpec((columns, PLANE), lambda i: (0, i)),
        ),
        compiler_params=pltpu.CompilerParams(vmem_limit_bytes=VMEM_LIMIT),
    )(rotation, *panels)
    return (filtered, rotated)


def solution(mesh):
    in_specs = (
        P("orb", "grid"),
        P("grid"),
        P("grid"),
        P("grid"),
        P("grid"),
        P(),
        P(None, None, "orb"),
        P(),
    )
    out_specs = (P("orb", "grid"), P("orb", "grid"))
    return jax.shard_map(body, mesh=mesh, in_specs=in_specs, out_specs=out_specs, check_vma=False)
```

```python
import functools

import jax
import jax.numpy as jnp
import numpy as np
from jax import lax
from jax.experimental import pallas as pl
from jax.experimental.pallas import tpu as pltpu
from jax.sharding import PartitionSpec as P

NX = 96
NY = 96
REACH = 6
ATOM_DEV = 4
PLANE = NX * NY
BLOCK_ROWS = 8
BLOCK = BLOCK_ROWS * NX
SLOTS = 16
TILE = 256
LANES = 128
CHUNKS = ((0, 12),)
VMEM_LIMIT = 24 * 2**20

stencil_weights = (
    -5369.0 / 1800.0,
    12.0 / 7.0,
    -15.0 / 56.0,
    10.0 / 189.0,
    -1.0 / 112.0,
    2.0 / 1925.0,
    -1.0 / 16632.0,
)
cheb_center = 6.0
cheb_half = 6.0

TAPS = {
    0: ((0, 0, 3), (1, 0, 3), (2, 0, 1)),
    1: ((0, 1, 3), (1, 0, 3), (2, 0, 2)),
    2: ((0, 2, 3), (1, 0, 3), (2, 0, 3)),
}


def plane_taps():
    cell = np.arange(BLOCK)
    row, column = cell // NX, cell % NX
    out = np.zeros((3, BLOCK, BLOCK), np.float64)
    for block in range(3):
        source_row = row + (block - 1) * BLOCK_ROWS
        jump_row = np.abs(source_row[:, None] - row[None, :])
        jump_column = np.abs(column[:, None] - column[None, :])
        for distance in range(1, REACH + 1):
            hit = ((jump_row == distance) & (jump_column == 0)) | (
                (jump_row == 0) & (jump_column == distance)
            )
            out[block][hit] = stencil_weights[distance] / stencil_weights[1]
    return out.astype(jnp.bfloat16)


def z_sum(planes, target, first):
    total = None
    for at, values in enumerate(planes):
        distance = abs(first + at - target)
        if 1 <= distance <= REACH:
            term = stencil_weights[distance] * values
            total = term if total is None else total + term
    return total


def block_diagonal(depth, rows, columns):
    row = lax.broadcasted_iota(jnp.int32, (depth * rows, depth * columns), 0) // rows
    column = lax.broadcasted_iota(jnp.int32, (depth * rows, depth * columns), 1) // columns
    return row == column


def split(values):
    high = values.astype(jnp.bfloat16)
    return high, (values - high.astype(jnp.float32)).astype(jnp.bfloat16)


def aligned(index, multiple):
    return pl.multiple_of(index, multiple)


class Sizes:
    def __init__(self, panel, cells, entries):
        self.panel, self.cells, self.entries = panel, cells, entries
        self.depth = cells // PLANE
        self.blocks = PLANE // BLOCK
        self.stride = self.depth * panel
        self.atoms = self.depth * SLOTS

    def chunk_cells(self, chunk):
        low, high = CHUNKS[chunk]
        return self.depth * (high - low) * BLOCK

    def start(self, plane, block, part=0):
        return aligned(plane * PLANE + block * BLOCK + part * TILE, LANES)

    def chunk_start(self, chunk, plane, block, part=0):
        low, high = CHUNKS[chunk]
        at = plane * (high - low) * BLOCK + (block - low) * BLOCK + part * TILE
        return aligned(at, LANES)

    def each_block(self, chunk, one):
        def step(block, carry):
            one(block)
            return carry

        lax.fori_loop(*CHUNKS[chunk], step, None)


def pack_planes(n, source, targets):
    zero = jnp.zeros((n.stride, BLOCK), jnp.bfloat16)
    for target in targets:
        target[0 : n.stride, :] = zero
        target[(n.blocks + 1) * n.stride : (n.blocks + 2) * n.stride, :] = zero

    def one(block, carry):
        for pair in range(n.depth // 2):
            halves = [
                source[:, pl.ds(n.start(plane, block), BLOCK)].astype(jnp.float32)
                for plane in (2 * pair, 2 * pair + 1)
            ]
            parts = split(jnp.concatenate(halves, axis=0))
            row = aligned((block + 1) * n.stride + pair * 2 * n.panel, 16)
            for target, part in zip(targets, parts):
                target[pl.ds(row, 2 * n.panel), :] = part
        return carry

    lax.fori_loop(0, n.blocks, one, None)


def apply_taps(n, packs, taps, out):
    rows = n.blocks * n.stride
    for tile, parts in TAPS.items():
        total = None
        for packed in packs:
            for block, low, high in parts:
                term = jnp.dot(
                    packed[block * n.stride : block * n.stride + rows, low * TILE : high * TILE],
                    taps[block, low * TILE : high * TILE, tile * TILE : (tile + 1) * TILE],
                    preferred_element_type=jnp.float32,
                )
                total = term if total is None else total + term
        out[:, tile * TILE : (tile + 1) * TILE] = total


def atom_partial(n, packs, table, out):
    total = None
    for block in range(n.blocks):
        weights = table[block * n.atoms : (block + 1) * n.atoms, :]
        for packed in packs:
            rows = packed[(block + 1) * n.stride : (block + 2) * n.stride, :]
            term = lax.dot_general(
                rows, weights, (((1,), (1,)), ((), ())), preferred_element_type=jnp.float32
            )
            total = term if total is None else total + term
    total = jnp.where(block_diagonal(n.depth, n.panel, SLOTS), total, 0.0)
    folded = total[0 : n.panel, :]
    for plane in range(1, n.depth):
        folded = folded + total[plane * n.panel : (plane + 1) * n.panel, :]
    slot = lax.broadcasted_iota(jnp.int32, (n.atoms, LANES), 0) % SLOTS
    lane = lax.broadcasted_iota(jnp.int32, (n.atoms, LANES), 1)
    out[...] = jnp.dot(
        folded,
        (slot == lane).astype(jnp.float32),
        precision=lax.Precision.HIGHEST,
        preferred_element_type=jnp.float32,
    )


def near_sums(n, tables, strength):
    own, partner, far, partner_far = tables
    outward = 2 * (lax.axis_index("grid") % 2) - 1
    slab = lax.axis_index("grid")
    total = own[...]
    for table, offset in (
        (partner[...], -outward),
        (far[0 : n.panel, :], outward),
        (far[n.panel : 2 * n.panel, :], 2 * outward),
        (partner_far[0 : n.panel, :], -2 * outward),
        (partner_far[n.panel : 2 * n.panel, :], -3 * outward),
    ):
        total = total + pltpu.roll(table, (offset * ATOM_DEV + LANES) % LANES, 1)
    count = strength.shape[1]
    atom = lax.broadcasted_iota(jnp.int32, (count, LANES), 0)
    slot = lax.broadcasted_iota(jnp.int32, (count, LANES), 1) + (slab - 1) * ATOM_DEV
    near = jnp.dot(
        jnp.broadcast_to(strength[...], (n.panel, count)),
        (atom == slot).astype(jnp.float32),
        precision=lax.Precision.HIGHEST,
        preferred_element_type=jnp.float32,
    )
    lane = lax.broadcasted_iota(jnp.int32, total.shape, 1)
    total = jnp.where(lane < 3 * ATOM_DEV, total * near, 0.0)
    slot = lax.broadcasted_iota(jnp.int32, (LANES, n.atoms), 1) % SLOTS
    lane = lax.broadcasted_iota(jnp.int32, (LANES, n.atoms), 0)
    return jnp.dot(
        total,
        (slot == lane).astype(jnp.float32),
        precision=lax.Precision.HIGHEST,
        preferred_element_type=jnp.float32,
    )


def by_side(inner, outer, run):
    odd = lax.axis_index("grid") % 2
    pl.when(odd == 0)(functools.partial(run, outer, inner))
    pl.when(odd == 1)(functools.partial(run, inner, outer))


def level_of(n, potential, plane, block, part):
    first = plane * (PLANE // LANES) + block * (BLOCK // LANES) + part * (TILE // LANES)
    return jnp.concatenate(
        [
            jnp.broadcast_to(potential[pl.ds(first + k, 1), :], (n.panel, LANES))
            for k in range(TILE // LANES)
        ],
        axis=1,
    )


def local_part(n, field, potential, sums, emit):
    for chunk in range(len(CHUNKS)):

        def one(block):
            for part in range(BLOCK // TILE):
                starts = [n.start(plane, block, part) for plane in range(n.depth)]
                planes = [field[:, pl.ds(start, TILE)].astype(jnp.float32) for start in starts]
                for plane in range(n.depth):
                    row = aligned(block * n.stride + plane * n.panel, 8)
                    lap = (
                        3.0 * stencil_weights[0] * planes[plane]
                        + stencil_weights[1]
                        * sums[pl.ds(row, n.panel), part * TILE : (part + 1) * TILE]
                        + z_sum(planes, plane, 0)
                    )
                    level = level_of(n, potential, plane, block, part)
                    value = -0.5 * lap + (level - cheb_center) * planes[plane]
                    emit(chunk, (plane, block, part), pl.ds(starts[plane], TILE), value)

        n.each_block(chunk, one)


def lap_beside(n, low, high, starts):
    below = [low[:, pl.ds(start, TILE)].astype(jnp.float32) for start in starts]
    above = [high[:, pl.ds(start, TILE)].astype(jnp.float32) for start in starts]
    return [
        z_sum(below, plane, -n.depth) + z_sum(above, plane, n.depth) for plane in range(n.depth)
    ]


def table_kernel(n, field, entry_ref, table, partial, packed, place):
    rows = n.entries // LANES

    def entry_row(first):
        return jnp.concatenate(
            [entry_ref[first * rows + k : first * rows + k + 1, :] for k in range(rows)], axis=1
        )

    row_at, lane_at = entry_row(0), entry_row(1)
    lane = lax.broadcasted_iota(jnp.int32, (BLOCK, n.entries), 0).astype(jnp.float32)
    place[...] = jnp.where(lane == lane_at, entry_row(2), 0.0).astype(jnp.bfloat16)
    chunk = 4 * n.atoms
    for first in range(0, n.blocks * n.atoms, chunk):
        row = lax.broadcasted_iota(jnp.int32, (chunk, n.entries), 0) + first
        hit = jnp.where(row.astype(jnp.float32) == row_at, 1.0, 0.0).astype(jnp.bfloat16)
        table[first : first + chunk, :] = lax.dot_general(
            hit, place[...], (((1,), (1,)), ((), ())), preferred_element_type=jnp.float32
        ).astype(jnp.bfloat16)
    pack_planes(n, field, (packed,))
    atom_partial(n, (packed,), table, partial)


def first_local_kernel(n, field, packed, potential, taps, out, sums):
    apply_taps(n, (packed,), taps, sums)

    def emit(chunk, tile, cells, value):
        out[:, cells] = value * (1.0 / cheb_half)

    local_part(n, field, potential, sums, emit)


def first_halo_kernel(n, local, inner, outer, table, strength, *refs):
    tables, out, sents = refs[:4], refs[4], refs[5:]
    wide = near_sums(n, tables, strength)
    rows = jnp.where(
        block_diagonal(n.depth, n.panel, SLOTS), jnp.concatenate([wide] * n.depth, axis=0), 0.0
    )
    rows = jnp.concatenate(split(rows), axis=1)

    def run(low, high):
        for chunk in range(len(CHUNKS)):

            def one(block):
                weights = table[pl.ds(aligned(block * n.atoms, 16), n.atoms), :]
                weights = jnp.concatenate([weights, weights], axis=0)
                spread = jnp.dot(rows, weights, preferred_element_type=jnp.float32)
                for part in range(BLOCK // TILE):
                    starts = [n.start(plane, block, part) for plane in range(n.depth)]
                    laps = lap_beside(n, low, high, starts)
                    for plane in range(n.depth):
                        near = spread[
                            plane * n.panel : (plane + 1) * n.panel,
                            part * TILE : (part + 1) * TILE,
                        ]
                        cells = pl.ds(starts[plane], TILE)
                        value = local[:, cells] + (near - 0.5 * laps[plane]) * (1.0 / cheb_half)
                        out[:, cells] = value
                        cells = pl.ds(n.chunk_start(chunk, plane, block, part), TILE)
                        sents[chunk][:, cells] = value.astype(jnp.bfloat16)

            n.each_block(chunk, one)

    by_side(inner, outer, run)


def second_sums_kernel(n, field, table, partial, packed, rest):
    pack_planes(n, field, (packed, rest))
    atom_partial(n, (packed, rest), table, partial)


def second_local_kernel(n, field, initial, packed, rest, potential, taps, *refs):
    *outs, sums = refs
    apply_taps(n, (packed, rest), taps, sums)

    def emit(chunk, tile, cells, value):
        value = value * (2.0 / cheb_half) - initial[:, cells].astype(jnp.float32)
        outs[chunk][:, pl.ds(n.chunk_start(chunk, *tile), TILE)] = value

    local_part(n, field, potential, sums, emit)


def second_halo_kernel(n, chunk, local, inner, outer, out, sent):
    def run(low, high):
        def one(block):
            for part in range(BLOCK // TILE):
                starts = [n.chunk_start(chunk, plane, block, part) for plane in range(n.depth)]
                laps = lap_beside(n, low, high, starts)
                for plane in range(n.depth):
                    cells = pl.ds(starts[plane], TILE)
                    value = local[:, cells] - laps[plane] * (1.0 / cheb_half)
                    out[:, cells] = value
                    sent[:, cells] = value.astype(jnp.bfloat16)

        n.each_block(chunk, one)

    by_side(inner, outer, run)


def atoms_kernel(n, strength, *refs):
    *tables, out = refs
    wide = near_sums(n, tables, strength) * (2.0 / cheb_half)
    out[...] = jnp.concatenate(
        [wide[:, 0:SLOTS], jnp.zeros((n.panel, LANES - SLOTS), jnp.float32)], axis=1
    )


def rotate_kernel(n, columns, rotation_ref, *refs):
    count = len(CHUNKS)
    *refs, table, filtered, rotated, rows_ref = refs
    orbs = len(refs) // (count + 1)
    adds, panels = refs[:orbs], refs[orbs:]
    rows = orbs * n.panel

    @pl.when(pl.program_id(0) == 0)
    def _():
        added = jnp.concatenate([add[...] for add in adds], axis=0)[:, 0:SLOTS]
        both = jnp.dot(
            rotation_ref[...],
            added,
            precision=lax.Precision.HIGHEST,
            preferred_element_type=jnp.float32,
        )
        top = jnp.concatenate([rotation_ref[...], both], axis=1)
        bottom = jnp.concatenate(
            [jnp.zeros((n.panel, rows), jnp.float32), added[0 : n.panel, :]], axis=1
        )
        rows_ref[...] = jnp.concatenate(split(jnp.concatenate([top, bottom], axis=0)), axis=1)

    plane = pl.program_id(0)
    size = columns + n.panel
    matrix = rows_ref[...]
    for chunk, (low, high) in enumerate(CHUNKS):
        for block in range(low, high):
            cut = pl.ds(n.chunk_start(chunk, plane, block), BLOCK)
            parts = [panel[:, cut].astype(jnp.float32) for panel in panels[chunk::count]]
            stack = jnp.concatenate(parts, axis=0).astype(jnp.bfloat16)
            atoms = table[pl.ds(aligned(block * n.atoms + plane * SLOTS, 16), SLOTS), :]
            stack = jnp.concatenate([stack, atoms] * 2, axis=0)
            both = jnp.dot(matrix, stack, preferred_element_type=jnp.float32)
            cells = slice(block * BLOCK, (block + 1) * BLOCK)
            filtered[:, cells] = (parts[0] + both[columns:size, :]).astype(jnp.bfloat16)
            rotated[:, cells] = both[0:columns, :].astype(jnp.bfloat16)


def call(kernel, out_shape, scratch, flops, *operands):
    bytes_accessed = sum(int(np.prod(o.shape)) * o.dtype.itemsize for o in operands)
    return pl.pallas_call(
        kernel,
        out_shape=out_shape,
        in_specs=[pl.BlockSpec(memory_space=pltpu.VMEM)] * len(operands),
        out_specs=jax.tree.map(lambda _: pl.BlockSpec(memory_space=pltpu.VMEM), out_shape),
        scratch_shapes=scratch,
        compiler_params=pltpu.CompilerParams(vmem_limit_bytes=VMEM_LIMIT),
        cost_estimate=pl.CostEstimate(
            flops=flops, bytes_accessed=bytes_accessed, transcendentals=0
        ),
    )(*operands)


def swapped(block, partner):
    count = lax.axis_size("grid")
    pairs = [(i, partner(i)) for i in range(count) if 0 <= partner(i) < count]
    return lax.ppermute(block, "grid", pairs)


def core_partner(i):
    return i ^ 1


def outer_partner(i):
    return i + 1 if i % 2 else i - 1


def exchange_sums(partial, after=None):
    partner = swapped(partial, core_partner)
    both = jnp.concatenate([partial, partner], axis=0)
    if after is not None:
        both, _ = lax.optimization_barrier((both, after))
    far = swapped(both, outer_partner)
    return partial, partner, far, swapped(far, core_partner)


def body(
    orbitals,
    potential,
    projector_atom,
    projector_cell,
    projector_value,
    atom_strength,
    ritz_rotation,
    panel_owner,
):
    panel, cells = orbitals.shape
    n = Sizes(panel, cells, projector_atom.shape[0])
    chunks = range(len(CHUNKS))
    taps = jnp.asarray(plane_taps())
    level = potential.reshape(n.cells // LANES, LANES)
    strength = atom_strength[None, :]

    bf16, f32 = jnp.bfloat16, jnp.float32
    shape = jax.ShapeDtypeStruct
    field = shape((panel, cells), f32)
    fields = [shape((panel, n.chunk_cells(chunk)), f32) for chunk in chunks]
    narrows = [shape((panel, n.chunk_cells(chunk)), bf16) for chunk in chunks]
    sums = shape((panel, LANES), f32)
    packed_shape = shape(((n.blocks + 2) * n.stride, BLOCK), bf16)
    tap_sums = pltpu.VMEM((n.blocks * n.stride, BLOCK), f32)

    inner, outer = swapped(orbitals, core_partner), swapped(orbitals, outer_partner)
    plane, inside = projector_cell // PLANE, projector_cell % PLANE
    slot = projector_atom - (lax.axis_index("grid") - 1) * ATOM_DEV
    row_at = ((inside // BLOCK) * n.depth + plane) * SLOTS + slot
    entries = jnp.concatenate(
        [
            entry.astype(f32).reshape(n.entries // LANES, LANES)
            for entry in (row_at, inside % BLOCK, projector_value)
        ],
        axis=0,
    )
    table, partial, packed = call(
        functools.partial(table_kernel, n),
        (shape((n.blocks * n.atoms, BLOCK), bf16), sums, packed_shape),
        [pltpu.VMEM((BLOCK, n.entries), bf16)],
        4 * 10**9,
        orbitals, entries,
    )
    local = call(
        functools.partial(first_local_kernel, n), field, [tap_sums], 2 * 10**9,
        orbitals, packed, level, taps,
    )
    near = exchange_sums(partial, local)
    step_field, *sents = call(
        functools.partial(first_halo_kernel, n),
        [field] + narrows, [], 10**9,
        local, inner, outer, table, strength, *near,
    )
    halos = [(swapped(sent, core_partner), swapped(sent, outer_partner)) for sent in sents]
    partial, packed, rest = call(
        functools.partial(second_sums_kernel, n),
        (sums, packed_shape, packed_shape), [], 10**9,
        step_field, table,
    )
    near = exchange_sums(partial)
    locals_ = call(
        functools.partial(second_local_kernel, n), fields, [tap_sums], 3 * 10**9,
        step_field, orbitals, packed, rest, level, taps,
    )

    orb_count = lax.axis_size("orb")

    def all_orbs(block):
        return [block] + [
            lax.ppermute(block, "orb", [(i, (i + k) % orb_count) for i in range(orb_count)])
            for k in range(1, orb_count)
        ]

    shares = []
    for chunk in chunks:
        own, sent = call(
            functools.partial(second_halo_kernel, n, chunk),
            (fields[chunk], narrows[chunk]), [], 10**9,
            locals_[chunk], *halos[chunk],
        )
        shares.append([own] + all_orbs(sent)[1:])
    added = call(functools.partial(atoms_kernel, n), sums, [], 10**6, strength, *near)
    adds = all_orbs(added)
    panels = [shares[chunk][k] for k in range(orb_count) for chunk in chunks]
    source = (lax.axis_index("orb") - jnp.arange(orb_count)) % orb_count
    chosen = (panel_owner[None, :] == source[:, None]).astype(f32)
    rotation = jnp.sum(
        chosen[:, :, None, None] * ritz_rotation.astype(f32)[None], axis=1
    )
    columns = ritz_rotation.shape[2]
    rotation = rotation.reshape(orb_count * panel, columns).T
    operands = (rotation, *adds, *panels, table)
    filtered, rotated = pl.pallas_call(
        functools.partial(rotate_kernel, n, columns),
        grid=(n.depth,),
        out_shape=(shape((panel, n.cells), bf16), shape((columns, n.cells), bf16)),
        in_specs=[pl.BlockSpec(memory_space=pltpu.VMEM)] * len(operands),
        out_specs=(
            pl.BlockSpec((panel, PLANE), lambda i: (0, i)),
            pl.BlockSpec((columns, PLANE), lambda i: (0, i)),
        ),
        scratch_shapes=[
            pltpu.VMEM((columns + panel, 2 * (orb_count * panel + SLOTS)), bf16)
        ],
        compiler_params=pltpu.CompilerParams(vmem_limit_bytes=VMEM_LIMIT),
    )(*operands)
    return (filtered, rotated)


def solution(mesh):
    in_specs = (
        P("orb", "grid"),
        P("grid"),
        P("grid"),
        P("grid"),
        P("grid"),
        P(),
        P(None, None, "orb"),
        P(),
    )
    out_specs = (P("orb", "grid"), P("orb", "grid"))
    return jax.shard_map(body, mesh=mesh, in_specs=in_specs, out_specs=out_specs, check_vma=False)
```

```python
import functools

import jax
import jax.numpy as jnp
import numpy as np
from jax import lax
from jax.experimental import pallas as pl
from jax.experimental.pallas import tpu as pltpu
from jax.sharding import PartitionSpec as P

NX = 96
NY = 96
REACH = 6
ATOM_DEV = 4
PLANE = NX * NY
BLOCK_ROWS = 8
BLOCK = BLOCK_ROWS * NX
SLOTS = 16
TILE = 256
LANES = 128
CHUNKS = ((0, 12),)
VMEM_LIMIT = 24 * 2**20

stencil_weights = (
    -5369.0 / 1800.0,
    12.0 / 7.0,
    -15.0 / 56.0,
    10.0 / 189.0,
    -1.0 / 112.0,
    2.0 / 1925.0,
    -1.0 / 16632.0,
)
cheb_center = 6.0
cheb_half = 6.0

TAPS = {
    0: ((0, 0, 3), (1, 0, 3), (2, 0, 1)),
    1: ((0, 1, 3), (1, 0, 3), (2, 0, 2)),
    2: ((0, 2, 3), (1, 0, 3), (2, 0, 3)),
}


def plane_taps():
    cell = np.arange(BLOCK)
    row, column = cell // NX, cell % NX
    out = np.zeros((3, BLOCK, BLOCK), np.float64)
    for block in range(3):
        source_row = row + (block - 1) * BLOCK_ROWS
        jump_row = np.abs(source_row[:, None] - row[None, :])
        jump_column = np.abs(column[:, None] - column[None, :])
        for distance in range(1, REACH + 1):
            hit = ((jump_row == distance) & (jump_column == 0)) | (
                (jump_row == 0) & (jump_column == distance)
            )
            out[block][hit] = stencil_weights[distance] / stencil_weights[1]
    return out.astype(jnp.bfloat16)


def z_sum(planes, target, first):
    total = None
    for at, values in enumerate(planes):
        distance = abs(first + at - target)
        if 1 <= distance <= REACH:
            term = stencil_weights[distance] * values
            total = term if total is None else total + term
    return total


def block_diagonal(depth, rows, columns):
    row = lax.broadcasted_iota(jnp.int32, (depth * rows, depth * columns), 0) // rows
    column = lax.broadcasted_iota(jnp.int32, (depth * rows, depth * columns), 1) // columns
    return row == column


def split(values):
    high = values.astype(jnp.bfloat16)
    return high, (values - high.astype(jnp.float32)).astype(jnp.bfloat16)


def aligned(index, multiple):
    return pl.multiple_of(index, multiple)


class Sizes:
    def __init__(self, panel, cells, entries):
        self.panel, self.cells, self.entries = panel, cells, entries
        self.depth = cells // PLANE
        self.blocks = PLANE // BLOCK
        self.stride = self.depth * panel
        self.atoms = self.depth * SLOTS

    def chunk_cells(self, chunk):
        low, high = CHUNKS[chunk]
        return self.depth * (high - low) * BLOCK

    def start(self, plane, block, part=0):
        return aligned(plane * PLANE + block * BLOCK + part * TILE, LANES)

    def chunk_start(self, chunk, plane, block, part=0):
        low, high = CHUNKS[chunk]
        at = plane * (high - low) * BLOCK + (block - low) * BLOCK + part * TILE
        return aligned(at, LANES)

    def each_block(self, chunk, one):
        def step(block, carry):
            one(block)
            return carry

        lax.fori_loop(*CHUNKS[chunk], step, None)


def pack_planes(n, source, targets):
    zero = jnp.zeros((n.stride, BLOCK), jnp.bfloat16)
    for target in targets:
        target[0 : n.stride, :] = zero
        target[(n.blocks + 1) * n.stride : (n.blocks + 2) * n.stride, :] = zero

    def one(block, carry):
        for pair in range(n.depth // 2):
            halves = [
                source[:, pl.ds(n.start(plane, block), BLOCK)].astype(jnp.float32)
                for plane in (2 * pair, 2 * pair + 1)
            ]
            parts = split(jnp.concatenate(halves, axis=0))
            row = aligned((block + 1) * n.stride + pair * 2 * n.panel, 16)
            for target, part in zip(targets, parts):
                target[pl.ds(row, 2 * n.panel), :] = part
        return carry

    lax.fori_loop(0, n.blocks, one, None)


def apply_taps(n, packs, taps, out):
    rows = n.blocks * n.stride
    for tile, parts in TAPS.items():
        total = None
        for packed in packs:
            for block, low, high in parts:
                term = jnp.dot(
                    packed[block * n.stride : block * n.stride + rows, low * TILE : high * TILE],
                    taps[block, low * TILE : high * TILE, tile * TILE : (tile + 1) * TILE],
                    preferred_element_type=jnp.float32,
                )
                total = term if total is None else total + term
        out[:, tile * TILE : (tile + 1) * TILE] = total


def atom_partial(n, packs, table, out):
    total = None
    for block in range(n.blocks):
        weights = table[block * n.atoms : (block + 1) * n.atoms, :]
        for packed in packs:
            rows = packed[(block + 1) * n.stride : (block + 2) * n.stride, :]
            term = lax.dot_general(
                rows, weights, (((1,), (1,)), ((), ())), preferred_element_type=jnp.float32
            )
            total = term if total is None else total + term
    total = jnp.where(block_diagonal(n.depth, n.panel, SLOTS), total, 0.0)
    folded = total[0 : n.panel, :]
    for plane in range(1, n.depth):
        folded = folded + total[plane * n.panel : (plane + 1) * n.panel, :]
    slot = lax.broadcasted_iota(jnp.int32, (n.atoms, LANES), 0) % SLOTS
    lane = lax.broadcasted_iota(jnp.int32, (n.atoms, LANES), 1)
    out[...] = jnp.dot(
        folded,
        (slot == lane).astype(jnp.float32),
        precision=lax.Precision.HIGHEST,
        preferred_element_type=jnp.float32,
    )


def near_sums(n, tables, strength):
    own, partner, far, partner_far = tables
    outward = 2 * (lax.axis_index("grid") % 2) - 1
    slab = lax.axis_index("grid")
    total = own[...]
    for table, offset in (
        (partner[...], -outward),
        (far[0 : n.panel, :], outward),
        (far[n.panel : 2 * n.panel, :], 2 * outward),
        (partner_far[0 : n.panel, :], -2 * outward),
        (partner_far[n.panel : 2 * n.panel, :], -3 * outward),
    ):
        total = total + pltpu.roll(table, (offset * ATOM_DEV + LANES) % LANES, 1)
    count = strength.shape[1]
    atom = lax.broadcasted_iota(jnp.int32, (count, LANES), 0)
    slot = lax.broadcasted_iota(jnp.int32, (count, LANES), 1) + (slab - 1) * ATOM_DEV
    near = jnp.dot(
        jnp.broadcast_to(strength[...], (n.panel, count)),
        (atom == slot).astype(jnp.float32),
        precision=lax.Precision.HIGHEST,
        preferred_element_type=jnp.float32,
    )
    lane = lax.broadcasted_iota(jnp.int32, total.shape, 1)
    total = jnp.where(lane < 3 * ATOM_DEV, total * near, 0.0)
    slot = lax.broadcasted_iota(jnp.int32, (LANES, n.atoms), 1) % SLOTS
    lane = lax.broadcasted_iota(jnp.int32, (LANES, n.atoms), 0)
    return jnp.dot(
        total,
        (slot == lane).astype(jnp.float32),
        precision=lax.Precision.HIGHEST,
        preferred_element_type=jnp.float32,
    )


def by_side(inner, outer, run):
    odd = lax.axis_index("grid") % 2
    pl.when(odd == 0)(functools.partial(run, outer, inner))
    pl.when(odd == 1)(functools.partial(run, inner, outer))


def level_of(n, potential, plane, block, part):
    first = plane * (PLANE // LANES) + block * (BLOCK // LANES) + part * (TILE // LANES)
    return jnp.concatenate(
        [
            jnp.broadcast_to(potential[pl.ds(first + k, 1), :], (n.panel, LANES))
            for k in range(TILE // LANES)
        ],
        axis=1,
    )


def local_part(n, field, potential, sums, emit):
    for chunk in range(len(CHUNKS)):

        def one(block):
            for part in range(BLOCK // TILE):
                starts = [n.start(plane, block, part) for plane in range(n.depth)]
                planes = [field[:, pl.ds(start, TILE)].astype(jnp.float32) for start in starts]
                for plane in range(n.depth):
                    row = aligned(block * n.stride + plane * n.panel, 8)
                    lap = (
                        3.0 * stencil_weights[0] * planes[plane]
                        + stencil_weights[1]
                        * sums[pl.ds(row, n.panel), part * TILE : (part + 1) * TILE]
                        + z_sum(planes, plane, 0)
                    )
                    level = level_of(n, potential, plane, block, part)
                    value = -0.5 * lap + (level - cheb_center) * planes[plane]
                    emit(chunk, (plane, block, part), pl.ds(starts[plane], TILE), value)

        n.each_block(chunk, one)


def lap_beside(n, low, high, starts):
    below = [low[:, pl.ds(start, TILE)].astype(jnp.float32) for start in starts]
    above = [high[:, pl.ds(start, TILE)].astype(jnp.float32) for start in starts]
    return [
        z_sum(below, plane, -n.depth) + z_sum(above, plane, n.depth) for plane in range(n.depth)
    ]


def table_kernel(n, field, entry_ref, table, partial, packed, place):
    rows = n.entries // LANES

    def entry_row(first):
        return jnp.concatenate(
            [entry_ref[first * rows + k : first * rows + k + 1, :] for k in range(rows)], axis=1
        )

    row_at, lane_at = entry_row(0), entry_row(1)
    lane = lax.broadcasted_iota(jnp.int32, (BLOCK, n.entries), 0).astype(jnp.float32)
    place[...] = jnp.where(lane == lane_at, entry_row(2), 0.0).astype(jnp.bfloat16)
    chunk = 4 * n.atoms
    for first in range(0, n.blocks * n.atoms, chunk):
        row = lax.broadcasted_iota(jnp.int32, (chunk, n.entries), 0) + first
        hit = jnp.where(row.astype(jnp.float32) == row_at, 1.0, 0.0).astype(jnp.bfloat16)
        table[first : first + chunk, :] = lax.dot_general(
            hit, place[...], (((1,), (1,)), ((), ())), preferred_element_type=jnp.float32
        ).astype(jnp.bfloat16)
    pack_planes(n, field, (packed,))
    atom_partial(n, (packed,), table, partial)


def first_local_kernel(n, field, packed, potential, taps, out, sums):
    apply_taps(n, (packed,), taps, sums)

    def emit(chunk, tile, cells, value):
        out[:, cells] = value * (1.0 / cheb_half)

    local_part(n, field, potential, sums, emit)


def first_halo_kernel(n, local, inner, outer, table, strength, *refs):
    tables, out, sents = refs[:4], refs[4], refs[5:]
    wide = near_sums(n, tables, strength)
    rows = jnp.where(
        block_diagonal(n.depth, n.panel, SLOTS), jnp.concatenate([wide] * n.depth, axis=0), 0.0
    )
    rows = jnp.concatenate(split(rows), axis=1)

    def run(low, high):
        for chunk in range(len(CHUNKS)):

            def one(block):
                weights = table[pl.ds(aligned(block * n.atoms, 16), n.atoms), :]
                weights = jnp.concatenate([weights, weights], axis=0)
                spread = jnp.dot(rows, weights, preferred_element_type=jnp.float32)
                for part in range(BLOCK // TILE):
                    starts = [n.start(plane, block, part) for plane in range(n.depth)]
                    laps = lap_beside(n, low, high, starts)
                    for plane in range(n.depth):
                        near = spread[
                            plane * n.panel : (plane + 1) * n.panel,
                            part * TILE : (part + 1) * TILE,
                        ]
                        cells = pl.ds(starts[plane], TILE)
                        value = local[:, cells] + (near - 0.5 * laps[plane]) * (1.0 / cheb_half)
                        out[:, cells] = value
                        cells = pl.ds(n.chunk_start(chunk, plane, block, part), TILE)
                        sents[chunk][:, cells] = value.astype(jnp.bfloat16)

            n.each_block(chunk, one)

    by_side(inner, outer, run)


def second_sums_kernel(n, field, table, partial, packed, rest):
    pack_planes(n, field, (packed, rest))
    atom_partial(n, (packed, rest), table, partial)


def second_local_kernel(n, field, initial, packed, rest, potential, taps, *refs):
    *outs, sums = refs
    apply_taps(n, (packed, rest), taps, sums)

    def emit(chunk, tile, cells, value):
        value = value * (2.0 / cheb_half) - initial[:, cells].astype(jnp.float32)
        outs[chunk][:, pl.ds(n.chunk_start(chunk, *tile), TILE)] = value

    local_part(n, field, potential, sums, emit)


def second_halo_kernel(n, chunk, local, inner, outer, out):
    def run(low, high):
        def one(block):
            for part in range(BLOCK // TILE):
                starts = [n.chunk_start(chunk, plane, block, part) for plane in range(n.depth)]
                laps = lap_beside(n, low, high, starts)
                for plane in range(n.depth):
                    cells = pl.ds(starts[plane], TILE)
                    value = local[:, cells] - laps[plane] * (1.0 / cheb_half)
                    out[:, cells] = value.astype(jnp.bfloat16)

        n.each_block(chunk, one)

    by_side(inner, outer, run)


def atoms_kernel(n, strength, *refs):
    *tables, out = refs
    wide = near_sums(n, tables, strength) * (2.0 / cheb_half)
    out[...] = jnp.concatenate(
        [wide[:, 0:SLOTS], jnp.zeros((n.panel, LANES - SLOTS), jnp.float32)], axis=1
    )


def weighted_rows(n, shifts, owner, ritz, added):
    columns = ritz.shape[1]
    blocks = []
    for shift in shifts:
        source = lax.axis_index("orb") + (lax.axis_size("orb") - shift)
        source = jnp.where(source >= lax.axis_size("orb"), source - lax.axis_size("orb"), source)
        total = jnp.zeros((n.panel, columns), jnp.float32)
        for step in range(ritz.shape[0] // n.panel):
            rows = ritz[step * n.panel : (step + 1) * n.panel, :].astype(jnp.float32)
            total = total + jnp.where(owner[step] == source, rows, 0.0)
        blocks.append(total)
    weights = jnp.concatenate(blocks, axis=0)
    eye = lax.broadcasted_iota(jnp.int32, (columns, columns), 0) == lax.broadcasted_iota(
        jnp.int32, (columns, columns), 1
    )
    rotation = lax.dot_general(
        eye.astype(jnp.float32),
        weights,
        (((1,), (1,)), ((), ())),
        precision=lax.Precision.HIGHEST,
        preferred_element_type=jnp.float32,
    )
    both = jnp.dot(
        rotation,
        added[:, 0:SLOTS],
        precision=lax.Precision.HIGHEST,
        preferred_element_type=jnp.float32,
    )
    return jnp.concatenate([rotation, both], axis=1)


def tile_rows(n, panels, table, plane, block):
    cells = pl.ds(n.start(plane, block), BLOCK)
    parts = [panel[:, cells].astype(jnp.float32) for panel in panels]
    stack = parts[0] if len(parts) == 1 else jnp.concatenate(parts, axis=0)
    atoms = table[pl.ds(aligned(block * n.atoms + plane * SLOTS, 16), SLOTS), :]
    stack = jnp.concatenate([stack, atoms.astype(jnp.float32)], axis=0).astype(jnp.bfloat16)
    return parts[0], stack


def rotate_own_kernel(n, owner, ritz, added, panel, table, filtered, rotated, rows_ref):
    columns = ritz.shape[1]

    @pl.when(pl.program_id(0) == 0)
    def _():
        top = weighted_rows(n, (0,), owner, ritz, added[...])
        bottom = jnp.concatenate(
            [jnp.zeros((n.panel, n.panel), jnp.float32), added[:, 0:SLOTS]], axis=1
        )
        rows_ref[...] = jnp.concatenate(split(jnp.concatenate([top, bottom], axis=0)), axis=1)

    plane = pl.program_id(0)
    matrix = rows_ref[...]
    for block in range(n.blocks):
        own, stack = tile_rows(n, (panel,), table, plane, block)
        both = jnp.dot(
            matrix,
            jnp.concatenate([stack, stack], axis=0),
            preferred_element_type=jnp.float32,
        )
        cells = slice(block * BLOCK, (block + 1) * BLOCK)
        filtered[:, cells] = (own + both[columns : columns + n.panel, :]).astype(jnp.bfloat16)
        rotated[:, pl.ds(n.start(plane, block), BLOCK)] = both[0:columns, :]


def rotate_rest_kernel(n, count, owner, ritz, *refs):
    *refs, own, table, rotated, rows_ref = refs
    adds, panels = refs[:count], refs[count:]

    @pl.when(pl.program_id(0) == 0)
    def _():
        added = jnp.concatenate([add[...] for add in adds], axis=0)
        rows = weighted_rows(n, range(1, count + 1), owner, ritz, added)
        rows_ref[...] = jnp.concatenate(split(rows), axis=1)

    plane = pl.program_id(0)
    matrix = rows_ref[...]
    for block in range(n.blocks):
        cells = pl.ds(n.start(plane, block), BLOCK)
        parts = [p[:, block * BLOCK : (block + 1) * BLOCK].astype(jnp.float32) for p in panels]
        atoms = table[pl.ds(aligned(block * n.atoms + plane * SLOTS, 16), SLOTS), :]
        parts.append(atoms.astype(jnp.float32))
        stack = jnp.concatenate(parts, axis=0).astype(jnp.bfloat16)
        total = own[:, cells] + jnp.dot(
            matrix,
            jnp.concatenate([stack, stack], axis=0),
            preferred_element_type=jnp.float32,
        )
        rotated[:, block * BLOCK : (block + 1) * BLOCK] = total.astype(jnp.bfloat16)


def call(kernel, out_shape, scratch, flops, *operands):
    bytes_accessed = sum(int(np.prod(o.shape)) * o.dtype.itemsize for o in operands)
    return pl.pallas_call(
        kernel,
        out_shape=out_shape,
        in_specs=[pl.BlockSpec(memory_space=pltpu.VMEM)] * len(operands),
        out_specs=jax.tree.map(lambda _: pl.BlockSpec(memory_space=pltpu.VMEM), out_shape),
        scratch_shapes=scratch,
        compiler_params=pltpu.CompilerParams(vmem_limit_bytes=VMEM_LIMIT),
        cost_estimate=pl.CostEstimate(
            flops=flops, bytes_accessed=bytes_accessed, transcendentals=0
        ),
    )(*operands)


def swapped(block, partner):
    count = lax.axis_size("grid")
    pairs = [(i, partner(i)) for i in range(count) if 0 <= partner(i) < count]
    return lax.ppermute(block, "grid", pairs)


def core_partner(i):
    return i ^ 1


def outer_partner(i):
    return i + 1 if i % 2 else i - 1


def exchange_sums(partial, after=None):
    partner = swapped(partial, core_partner)
    both = jnp.concatenate([partial, partner], axis=0)
    if after is not None:
        both, _ = lax.optimization_barrier((both, after))
    far = swapped(both, outer_partner)
    return partial, partner, far, swapped(far, core_partner)


def body(
    orbitals,
    potential,
    projector_atom,
    projector_cell,
    projector_value,
    atom_strength,
    ritz_rotation,
    panel_owner,
):
    panel, cells = orbitals.shape
    n = Sizes(panel, cells, projector_atom.shape[0])
    chunks = range(len(CHUNKS))
    taps = jnp.asarray(plane_taps())
    level = potential.reshape(n.cells // LANES, LANES)
    strength = atom_strength[None, :]

    bf16, f32 = jnp.bfloat16, jnp.float32
    shape = jax.ShapeDtypeStruct
    field = shape((panel, cells), f32)
    fields = [shape((panel, n.chunk_cells(chunk)), f32) for chunk in chunks]
    narrows = [shape((panel, n.chunk_cells(chunk)), bf16) for chunk in chunks]
    sums = shape((panel, LANES), f32)
    packed_shape = shape(((n.blocks + 2) * n.stride, BLOCK), bf16)
    tap_sums = pltpu.VMEM((n.blocks * n.stride, BLOCK), f32)

    inner, outer = swapped(orbitals, core_partner), swapped(orbitals, outer_partner)
    plane, inside = projector_cell // PLANE, projector_cell % PLANE
    slot = projector_atom - (lax.axis_index("grid") - 1) * ATOM_DEV
    row_at = ((inside // BLOCK) * n.depth + plane) * SLOTS + slot
    entries = jnp.concatenate(
        [
            entry.astype(f32).reshape(n.entries // LANES, LANES)
            for entry in (row_at, inside % BLOCK, projector_value)
        ],
        axis=0,
    )
    table, partial, packed = call(
        functools.partial(table_kernel, n),
        (shape((n.blocks * n.atoms, BLOCK), bf16), sums, packed_shape),
        [pltpu.VMEM((BLOCK, n.entries), bf16)],
        4 * 10**9,
        orbitals, entries,
    )
    local = call(
        functools.partial(first_local_kernel, n), field, [tap_sums], 2 * 10**9,
        orbitals, packed, level, taps,
    )
    near = exchange_sums(partial, local)
    step_field, *sents = call(
        functools.partial(first_halo_kernel, n),
        [field] + narrows, [], 10**9,
        local, inner, outer, table, strength, *near,
    )
    halos = [(swapped(sent, core_partner), swapped(sent, outer_partner)) for sent in sents]
    partial, packed, rest = call(
        functools.partial(second_sums_kernel, n),
        (sums, packed_shape, packed_shape), [], 10**9,
        step_field, table,
    )
    locals_ = call(
        functools.partial(second_local_kernel, n), fields, [tap_sums], 3 * 10**9,
        step_field, orbitals, packed, rest, level, taps,
    )

    orb_count = lax.axis_size("orb")

    def all_orbs(block):
        return [block] + [
            lax.ppermute(block, "orb", [(i, (i + k) % orb_count) for i in range(orb_count)])
            for k in range(1, orb_count)
        ]

    near = exchange_sums(partial)
    held, _ = lax.optimization_barrier((locals_[0], near[2]))
    share = call(
        functools.partial(second_halo_kernel, n, 0), narrows[0], [], 10**9,
        held, *halos[0],
    )
    panels = all_orbs(share)
    added = call(functools.partial(atoms_kernel, n), sums, [], 10**6, strength, *near)
    adds = all_orbs(added)
    columns = ritz_rotation.shape[2]
    ritz = ritz_rotation.reshape(-1, columns)
    smem = pl.BlockSpec(memory_space=pltpu.SMEM)
    vmem = pl.BlockSpec(memory_space=pltpu.VMEM)
    plane_of = lambda rows: pl.BlockSpec((rows, PLANE), lambda i: (0, i))
    params = pltpu.CompilerParams(vmem_limit_bytes=VMEM_LIMIT)
    filtered, rotated = pl.pallas_call(
        functools.partial(rotate_own_kernel, n),
        grid=(n.depth,),
        out_shape=(shape((panel, n.cells), bf16), shape((columns, n.cells), f32)),
        in_specs=[smem] + [vmem] * 4,
        out_specs=(plane_of(panel), vmem),
        scratch_shapes=[pltpu.VMEM((columns + panel, 2 * (panel + SLOTS)), bf16)],
        compiler_params=params,
    )(panel_owner, ritz, adds[0], share, table)
    rest = orb_count - 1
    rotated = pl.pallas_call(
        functools.partial(rotate_rest_kernel, n, rest),
        grid=(n.depth,),
        out_shape=shape((columns, n.cells), bf16),
        in_specs=[smem] + [vmem] * (1 + rest) + [plane_of(panel)] * rest + [vmem] * 2,
        out_specs=plane_of(columns),
        scratch_shapes=[pltpu.VMEM((columns, 2 * (rest * panel + SLOTS)), bf16)],
        compiler_params=params,
    )(panel_owner, ritz, *adds[1:], *panels[1:], rotated, table)
    return (filtered, rotated)


def solution(mesh):
    in_specs = (
        P("orb", "grid"),
        P("grid"),
        P("grid"),
        P("grid"),
        P("grid"),
        P(),
        P(None, None, "orb"),
        P(),
    )
    out_specs = (P("orb", "grid"), P("orb", "grid"))
    return jax.shard_map(body, mesh=mesh, in_specs=in_specs, out_specs=out_specs, check_vma=False)
```

```python
import functools

import jax
import jax.numpy as jnp
import numpy as np
from jax import lax
from jax.experimental import pallas as pl
from jax.experimental.pallas import tpu as pltpu
from jax.sharding import PartitionSpec as P

NX = 96
NY = 96
REACH = 6
ATOM_DEV = 4
PLANE = NX * NY
BLOCK_ROWS = 8
BLOCK = BLOCK_ROWS * NX
SLOTS = 16
TILE = 256
LANES = 128
CHUNKS = ((0, 12),)
VMEM_LIMIT = 24 * 2**20

stencil_weights = (
    -5369.0 / 1800.0,
    12.0 / 7.0,
    -15.0 / 56.0,
    10.0 / 189.0,
    -1.0 / 112.0,
    2.0 / 1925.0,
    -1.0 / 16632.0,
)
cheb_center = 6.0
cheb_half = 6.0

TAPS = {
    0: ((0, 0, 3), (1, 0, 3), (2, 0, 1)),
    1: ((0, 1, 3), (1, 0, 3), (2, 0, 2)),
    2: ((0, 2, 3), (1, 0, 3), (2, 0, 3)),
}


def plane_taps():
    cell = np.arange(BLOCK)
    row, column = cell // NX, cell % NX
    out = np.zeros((3, BLOCK, BLOCK), np.float64)
    for block in range(3):
        source_row = row + (block - 1) * BLOCK_ROWS
        jump_row = np.abs(source_row[:, None] - row[None, :])
        jump_column = np.abs(column[:, None] - column[None, :])
        for distance in range(1, REACH + 1):
            hit = ((jump_row == distance) & (jump_column == 0)) | (
                (jump_row == 0) & (jump_column == distance)
            )
            out[block][hit] = stencil_weights[distance] / stencil_weights[1]
    return out.astype(jnp.bfloat16)


def z_sum(planes, target, first):
    total = None
    for at, values in enumerate(planes):
        distance = abs(first + at - target)
        if 1 <= distance <= REACH:
            term = stencil_weights[distance] * values
            total = term if total is None else total + term
    return total


def block_diagonal(depth, rows, columns):
    row = lax.broadcasted_iota(jnp.int32, (depth * rows, depth * columns), 0) // rows
    column = lax.broadcasted_iota(jnp.int32, (depth * rows, depth * columns), 1) // columns
    return row == column


def split(values):
    high = values.astype(jnp.bfloat16)
    return high, (values - high.astype(jnp.float32)).astype(jnp.bfloat16)


def aligned(index, multiple):
    return pl.multiple_of(index, multiple)


class Sizes:
    def __init__(self, panel, cells, entries):
        self.panel, self.cells, self.entries = panel, cells, entries
        self.depth = cells // PLANE
        self.blocks = PLANE // BLOCK
        self.stride = self.depth * panel
        self.atoms = self.depth * SLOTS

    def chunk_cells(self, chunk):
        low, high = CHUNKS[chunk]
        return self.depth * (high - low) * BLOCK

    def start(self, plane, block, part=0):
        return aligned(plane * PLANE + block * BLOCK + part * TILE, LANES)

    def chunk_start(self, chunk, plane, block, part=0):
        low, high = CHUNKS[chunk]
        at = plane * (high - low) * BLOCK + (block - low) * BLOCK + part * TILE
        return aligned(at, LANES)

    def each_block(self, chunk, one):
        def step(block, carry):
            one(block)
            return carry

        lax.fori_loop(*CHUNKS[chunk], step, None, unroll=2)


def pack_planes(n, source, targets):
    zero = jnp.zeros((n.stride, BLOCK), jnp.bfloat16)
    for target in targets:
        target[0 : n.stride, :] = zero
        target[(n.blocks + 1) * n.stride : (n.blocks + 2) * n.stride, :] = zero

    def one(block, carry):
        for pair in range(n.depth // 2):
            halves = [
                source[:, pl.ds(n.start(plane, block), BLOCK)].astype(jnp.float32)
                for plane in (2 * pair, 2 * pair + 1)
            ]
            parts = split(jnp.concatenate(halves, axis=0))
            row = aligned((block + 1) * n.stride + pair * 2 * n.panel, 16)
            for target, part in zip(targets, parts):
                target[pl.ds(row, 2 * n.panel), :] = part
        return carry

    lax.fori_loop(0, n.blocks, one, None)


def apply_taps(n, packs, taps, out):
    rows = n.blocks * n.stride
    for tile, parts in TAPS.items():
        total = None
        for packed in packs:
            for block, low, high in parts:
                term = jnp.dot(
                    packed[block * n.stride : block * n.stride + rows, low * TILE : high * TILE],
                    taps[block, low * TILE : high * TILE, tile * TILE : (tile + 1) * TILE],
                    preferred_element_type=jnp.float32,
                )
                total = term if total is None else total + term
        out[:, tile * TILE : (tile + 1) * TILE] = total


def atom_partial(n, packs, table, out):
    total = None
    for block in range(n.blocks):
        weights = table[block * n.atoms : (block + 1) * n.atoms, :]
        for packed in packs:
            rows = packed[(block + 1) * n.stride : (block + 2) * n.stride, :]
            term = lax.dot_general(
                rows, weights, (((1,), (1,)), ((), ())), preferred_element_type=jnp.float32
            )
            total = term if total is None else total + term
    total = jnp.where(block_diagonal(n.depth, n.panel, SLOTS), total, 0.0)
    folded = total[0 : n.panel, :]
    for plane in range(1, n.depth):
        folded = folded + total[plane * n.panel : (plane + 1) * n.panel, :]
    wide = jnp.concatenate([folded, jnp.zeros((n.panel, LANES - n.atoms), jnp.float32)], axis=1)
    total = wide
    for plane in range(1, n.depth):
        total = total + pltpu.roll(wide, LANES - plane * SLOTS, 1)
    lane = lax.broadcasted_iota(jnp.int32, total.shape, 1)
    out[...] = jnp.where(lane < SLOTS, total, 0.0)


def near_sums(n, tables, strength):
    own, partner, far, partner_far = tables
    outward = 2 * (lax.axis_index("grid") % 2) - 1
    slab = lax.axis_index("grid")
    total = own[...]
    for table, offset in (
        (partner[...], -outward),
        (far[0 : n.panel, :], outward),
        (far[n.panel : 2 * n.panel, :], 2 * outward),
        (partner_far[0 : n.panel, :], -2 * outward),
        (partner_far[n.panel : 2 * n.panel, :], -3 * outward),
    ):
        total = total + pltpu.roll(table, (offset * ATOM_DEV + LANES) % LANES, 1)
    count = strength.shape[1]
    near = strength[...]
    if count < LANES:
        near = jnp.concatenate([near, jnp.zeros((1, LANES - count), jnp.float32)], axis=1)
    near = jnp.broadcast_to(near, total.shape)
    near = pltpu.roll(near, (ATOM_DEV - slab * ATOM_DEV + LANES) % LANES, 1)
    lane = lax.broadcasted_iota(jnp.int32, total.shape, 1)
    return jnp.where(lane < 3 * ATOM_DEV, total * near, 0.0)


def on_planes(n, sums):
    wide = sums
    for plane in range(1, n.depth):
        wide = wide + pltpu.roll(sums, plane * SLOTS, 1)
    return wide[:, 0 : n.atoms]


def by_side(inner, outer, run):
    odd = lax.axis_index("grid") % 2
    pl.when(odd == 0)(functools.partial(run, outer, inner))
    pl.when(odd == 1)(functools.partial(run, inner, outer))


def level_of(n, potential, plane, block, part):
    first = plane * (PLANE // LANES) + block * (BLOCK // LANES) + part * (TILE // LANES)
    return jnp.concatenate(
        [
            jnp.broadcast_to(potential[pl.ds(first + k, 1), :], (n.panel, LANES))
            for k in range(TILE // LANES)
        ],
        axis=1,
    )


def local_part(n, field, potential, sums, emit):
    for chunk in range(len(CHUNKS)):

        def one(block):
            for part in range(BLOCK // TILE):
                starts = [n.start(plane, block, part) for plane in range(n.depth)]
                planes = [field[:, pl.ds(start, TILE)].astype(jnp.float32) for start in starts]
                for plane in range(n.depth):
                    row = aligned(block * n.stride + plane * n.panel, 8)
                    lap = (
                        3.0 * stencil_weights[0] * planes[plane]
                        + stencil_weights[1]
                        * sums[pl.ds(row, n.panel), part * TILE : (part + 1) * TILE]
                        + z_sum(planes, plane, 0)
                    )
                    level = level_of(n, potential, plane, block, part)
                    value = -0.5 * lap + (level - cheb_center) * planes[plane]
                    emit(chunk, (plane, block, part), pl.ds(starts[plane], TILE), value)

        n.each_block(chunk, one)


def lap_beside(n, low, high, starts):
    below = [low[:, pl.ds(start, TILE)].astype(jnp.float32) for start in starts]
    above = [high[:, pl.ds(start, TILE)].astype(jnp.float32) for start in starts]
    return [
        z_sum(below, plane, -n.depth) + z_sum(above, plane, n.depth) for plane in range(n.depth)
    ]


def table_kernel(n, field, entry_ref, table, partial, packed, place):
    rows = n.entries // LANES

    def entry_row(first):
        return jnp.concatenate(
            [entry_ref[first * rows + k : first * rows + k + 1, :] for k in range(rows)], axis=1
        )

    row_at, lane_at = entry_row(0), entry_row(1)
    lane = lax.broadcasted_iota(jnp.int32, (BLOCK, n.entries), 0).astype(jnp.float32)
    place[...] = jnp.where(lane == lane_at, entry_row(2), 0.0).astype(jnp.bfloat16)
    chunk = 4 * n.atoms
    for first in range(0, n.blocks * n.atoms, chunk):
        row = lax.broadcasted_iota(jnp.int32, (chunk, n.entries), 0) + first
        hit = jnp.where(row.astype(jnp.float32) == row_at, 1.0, 0.0).astype(jnp.bfloat16)
        table[first : first + chunk, :] = lax.dot_general(
            hit, place[...], (((1,), (1,)), ((), ())), preferred_element_type=jnp.float32
        ).astype(jnp.bfloat16)
    pack_planes(n, field, (packed,))
    atom_partial(n, (packed,), table, partial)


def first_local_kernel(n, field, packed, potential, taps, out, sums):
    apply_taps(n, (packed,), taps, sums)

    def emit(chunk, tile, cells, value):
        out[:, cells] = value * (1.0 / cheb_half)

    local_part(n, field, potential, sums, emit)


def first_halo_kernel(n, local, inner, outer, table, strength, *refs):
    tables, out, sents = refs[:4], refs[4], refs[5:]
    wide = on_planes(n, near_sums(n, tables, strength))
    rows = jnp.where(
        block_diagonal(n.depth, n.panel, SLOTS), jnp.concatenate([wide] * n.depth, axis=0), 0.0
    )
    rows = jnp.concatenate(split(rows), axis=1)

    def run(low, high):
        for chunk in range(len(CHUNKS)):

            def one(block):
                weights = table[pl.ds(aligned(block * n.atoms, 16), n.atoms), :]
                weights = jnp.concatenate([weights, weights], axis=0)
                spread = jnp.dot(rows, weights, preferred_element_type=jnp.float32)
                for part in range(BLOCK // TILE):
                    starts = [n.start(plane, block, part) for plane in range(n.depth)]
                    laps = lap_beside(n, low, high, starts)
                    for plane in range(n.depth):
                        near = spread[
                            plane * n.panel : (plane + 1) * n.panel,
                            part * TILE : (part + 1) * TILE,
                        ]
                        cells = pl.ds(starts[plane], TILE)
                        value = local[:, cells] + (near - 0.5 * laps[plane]) * (1.0 / cheb_half)
                        out[:, cells] = value
                        cells = pl.ds(n.chunk_start(chunk, plane, block, part), TILE)
                        sents[chunk][:, cells] = value.astype(jnp.bfloat16)

            n.each_block(chunk, one)

    by_side(inner, outer, run)


def second_sums_kernel(n, field, table, partial, packed, rest):
    pack_planes(n, field, (packed, rest))
    atom_partial(n, (packed, rest), table, partial)


def second_local_kernel(n, field, initial, packed, rest, potential, taps, *refs):
    *outs, sums = refs
    apply_taps(n, (packed, rest), taps, sums)

    def emit(chunk, tile, cells, value):
        value = value * (2.0 / cheb_half) - initial[:, cells].astype(jnp.float32)
        outs[chunk][:, pl.ds(n.chunk_start(chunk, *tile), TILE)] = value

    local_part(n, field, potential, sums, emit)


def second_halo_kernel(n, chunk, local, inner, outer, out):
    def run(low, high):
        def one(block):
            for part in range(BLOCK // TILE):
                starts = [n.chunk_start(chunk, plane, block, part) for plane in range(n.depth)]
                laps = lap_beside(n, low, high, starts)
                for plane in range(n.depth):
                    cells = pl.ds(starts[plane], TILE)
                    value = local[:, cells] - laps[plane] * (1.0 / cheb_half)
                    out[:, cells] = value.astype(jnp.bfloat16)

        n.each_block(chunk, one)

    by_side(inner, outer, run)


def atoms_kernel(n, strength, *refs):
    *tables, out = refs
    out[...] = near_sums(n, tables, strength) * (2.0 / cheb_half)


def rotation_rows(n, shifts, owner, ritz):
    columns = ritz.shape[1]
    blocks = []
    for shift in shifts:
        source = lax.axis_index("orb") + (lax.axis_size("orb") - shift)
        source = jnp.where(source >= lax.axis_size("orb"), source - lax.axis_size("orb"), source)
        total = jnp.zeros((n.panel, columns), jnp.float32)
        for step in range(ritz.shape[0] // n.panel):
            rows = ritz[step * n.panel : (step + 1) * n.panel, :].astype(jnp.float32)
            total = total + jnp.where(owner[step] == source, rows, 0.0)
        blocks.append(total)
    weights = jnp.concatenate(blocks, axis=0)
    eye = lax.broadcasted_iota(jnp.int32, (columns, columns), 0) == lax.broadcasted_iota(
        jnp.int32, (columns, columns), 1
    )
    return lax.dot_general(
        eye.astype(jnp.float32),
        weights,
        (((1,), (1,)), ((), ())),
        precision=lax.Precision.HIGHEST,
        preferred_element_type=jnp.float32,
    )


def with_slots(rotation, added):
    both = jnp.dot(
        rotation,
        added[:, 0:SLOTS],
        precision=lax.Precision.HIGHEST,
        preferred_element_type=jnp.float32,
    )
    return jnp.concatenate([rotation, both], axis=1)


def tile_rows(n, panels, table, plane, block):
    cells = pl.ds(n.start(plane, block), BLOCK)
    parts = [panel[:, cells].astype(jnp.float32) for panel in panels]
    stack = parts[0] if len(parts) == 1 else jnp.concatenate(parts, axis=0)
    atoms = table[pl.ds(aligned(block * n.atoms + plane * SLOTS, 16), SLOTS), :]
    stack = jnp.concatenate([stack, atoms.astype(jnp.float32)], axis=0).astype(jnp.bfloat16)
    return parts[0], stack


def rotate_own_kernel(
    n, orbs, owner, ritz, added, panel, table, filtered, rotated, rest, rows_ref
):
    columns = ritz.shape[1]

    @pl.when(pl.program_id(0) == 0)
    def _():
        rotation = rotation_rows(n, range(orbs), owner, ritz)
        rest[...] = rotation[:, n.panel :]
        top = with_slots(rotation[:, 0 : n.panel], added[...])
        bottom = jnp.concatenate(
            [jnp.zeros((n.panel, n.panel), jnp.float32), added[:, 0:SLOTS]], axis=1
        )
        rows_ref[...] = jnp.concatenate(split(jnp.concatenate([top, bottom], axis=0)), axis=1)

    plane = pl.program_id(0)
    matrix = rows_ref[...]
    for block in range(n.blocks):
        own, stack = tile_rows(n, (panel,), table, plane, block)
        both = jnp.dot(
            matrix,
            jnp.concatenate([stack, stack], axis=0),
            preferred_element_type=jnp.float32,
        )
        cells = slice(block * BLOCK, (block + 1) * BLOCK)
        filtered[:, cells] = (own + both[columns : columns + n.panel, :]).astype(jnp.bfloat16)
        rotated[:, pl.ds(n.start(plane, block), BLOCK)] = both[0:columns, :]


def rotate_rest_kernel(n, count, rotation, *refs):
    *refs, own, table, rotated, rows_ref = refs
    adds, panels = refs[:count], refs[count:]

    @pl.when(pl.program_id(0) == 0)
    def _():
        added = jnp.concatenate([add[...] for add in adds], axis=0)
        rows_ref[...] = jnp.concatenate(split(with_slots(rotation[...], added)), axis=1)

    plane = pl.program_id(0)
    matrix = rows_ref[...]
    for block in range(n.blocks):
        cells = pl.ds(n.start(plane, block), BLOCK)
        parts = [p[:, block * BLOCK : (block + 1) * BLOCK].astype(jnp.float32) for p in panels]
        atoms = table[pl.ds(aligned(block * n.atoms + plane * SLOTS, 16), SLOTS), :]
        parts.append(atoms.astype(jnp.float32))
        stack = jnp.concatenate(parts, axis=0).astype(jnp.bfloat16)
        total = own[:, cells] + jnp.dot(
            matrix,
            jnp.concatenate([stack, stack], axis=0),
            preferred_element_type=jnp.float32,
        )
        rotated[:, block * BLOCK : (block + 1) * BLOCK] = total.astype(jnp.bfloat16)


def call(kernel, out_shape, scratch, flops, *operands):
    bytes_accessed = sum(int(np.prod(o.shape)) * o.dtype.itemsize for o in operands)
    return pl.pallas_call(
        kernel,
        out_shape=out_shape,
        in_specs=[pl.BlockSpec(memory_space=pltpu.VMEM)] * len(operands),
        out_specs=jax.tree.map(lambda _: pl.BlockSpec(memory_space=pltpu.VMEM), out_shape),
        scratch_shapes=scratch,
        compiler_params=pltpu.CompilerParams(vmem_limit_bytes=VMEM_LIMIT),
        cost_estimate=pl.CostEstimate(
            flops=flops, bytes_accessed=bytes_accessed, transcendentals=0
        ),
    )(*operands)


def swapped(block, partner):
    count = lax.axis_size("grid")
    pairs = [(i, partner(i)) for i in range(count) if 0 <= partner(i) < count]
    return lax.ppermute(block, "grid", pairs)


def core_partner(i):
    return i ^ 1


def outer_partner(i):
    return i + 1 if i % 2 else i - 1


def exchange_sums(partial, after=None):
    partner = swapped(partial, core_partner)
    both = jnp.concatenate([partial, partner], axis=0)
    if after is not None:
        both, _ = lax.optimization_barrier((both, after))
    far = swapped(both, outer_partner)
    return partial, partner, far, swapped(far, core_partner)


def body(
    orbitals,
    potential,
    projector_atom,
    projector_cell,
    projector_value,
    atom_strength,
    ritz_rotation,
    panel_owner,
):
    panel, cells = orbitals.shape
    n = Sizes(panel, cells, projector_atom.shape[0])
    chunks = range(len(CHUNKS))
    taps = jnp.asarray(plane_taps())
    level = potential.reshape(n.cells // LANES, LANES)
    strength = atom_strength[None, :]

    bf16, f32 = jnp.bfloat16, jnp.float32
    shape = jax.ShapeDtypeStruct
    field = shape((panel, cells), f32)
    fields = [shape((panel, n.chunk_cells(chunk)), f32) for chunk in chunks]
    narrows = [shape((panel, n.chunk_cells(chunk)), bf16) for chunk in chunks]
    sums = shape((panel, LANES), f32)
    packed_shape = shape(((n.blocks + 2) * n.stride, BLOCK), bf16)
    tap_sums = pltpu.VMEM((n.blocks * n.stride, BLOCK), f32)

    outer = swapped(orbitals, outer_partner)
    inner = swapped(orbitals, core_partner)
    plane, inside = projector_cell // PLANE, projector_cell % PLANE
    slot = projector_atom - (lax.axis_index("grid") - 1) * ATOM_DEV
    row_at = ((inside // BLOCK) * n.depth + plane) * SLOTS + slot
    entries = jnp.concatenate(
        [
            entry.astype(f32).reshape(n.entries // LANES, LANES)
            for entry in (row_at, inside % BLOCK, projector_value)
        ],
        axis=0,
    )
    table, partial, packed = call(
        functools.partial(table_kernel, n),
        (shape((n.blocks * n.atoms, BLOCK), bf16), sums, packed_shape),
        [pltpu.VMEM((BLOCK, n.entries), bf16)],
        4 * 10**9,
        orbitals, entries,
    )
    local = call(
        functools.partial(first_local_kernel, n), field, [tap_sums], 2 * 10**9,
        orbitals, packed, level, taps,
    )
    near = exchange_sums(partial, local)
    step_field, *sents = call(
        functools.partial(first_halo_kernel, n),
        [field] + narrows, [], 10**9,
        local, inner, outer, table, strength, *near,
    )
    outers = [swapped(sent, outer_partner) for sent in sents]
    halos = [(swapped(sent, core_partner), outer) for sent, outer in zip(sents, outers)]
    partial, packed, rest = call(
        functools.partial(second_sums_kernel, n),
        (sums, packed_shape, packed_shape), [], 10**9,
        step_field, table,
    )
    locals_ = call(
        functools.partial(second_local_kernel, n), fields, [tap_sums], 3 * 10**9,
        step_field, orbitals, packed, rest, level, taps,
    )

    orb_count = lax.axis_size("orb")

    def all_orbs(block):
        return [block] + [
            lax.ppermute(block, "orb", [(i, (i + k) % orb_count) for i in range(orb_count)])
            for k in range(1, orb_count)
        ]

    near = exchange_sums(partial)
    held, _ = lax.optimization_barrier((locals_[0], near[2]))
    share = call(
        functools.partial(second_halo_kernel, n, 0), narrows[0], [], 10**9,
        held, *halos[0],
    )
    panels = all_orbs(share)
    added = call(functools.partial(atoms_kernel, n), sums, [], 10**6, strength, *near)
    adds = all_orbs(added)
    columns = ritz_rotation.shape[2]
    ritz = ritz_rotation.reshape(-1, columns)
    smem = pl.BlockSpec(memory_space=pltpu.SMEM)
    vmem = pl.BlockSpec(memory_space=pltpu.VMEM)
    plane_of = lambda rows: pl.BlockSpec((rows, PLANE), lambda i: (0, i))
    params = pltpu.CompilerParams(vmem_limit_bytes=VMEM_LIMIT)
    rest = orb_count - 1
    filtered, rotated, rotation = pl.pallas_call(
        functools.partial(rotate_own_kernel, n, orb_count),
        grid=(n.depth,),
        out_shape=(
            shape((panel, n.cells), bf16),
            shape((columns, n.cells), f32),
            shape((columns, rest * panel), f32),
        ),
        in_specs=[smem] + [vmem] * 4,
        out_specs=(plane_of(panel), vmem, vmem),
        scratch_shapes=[pltpu.VMEM((columns + panel, 2 * (panel + SLOTS)), bf16)],
        compiler_params=params,
    )(panel_owner, ritz, adds[0], share, table)
    rotated = pl.pallas_call(
        functools.partial(rotate_rest_kernel, n, rest),
        grid=(n.depth,),
        out_shape=shape((columns, n.cells), bf16),
        in_specs=[vmem] * (1 + rest) + [plane_of(panel)] * rest + [vmem] * 2,
        out_specs=plane_of(columns),
        scratch_shapes=[pltpu.VMEM((columns, 2 * (rest * panel + SLOTS)), bf16)],
        compiler_params=params,
    )(rotation, *adds[1:], *panels[1:], rotated, table)
    return (filtered, rotated)


def solution(mesh):
    in_specs = (
        P("orb", "grid"),
        P("grid"),
        P("grid"),
        P("grid"),
        P("grid"),
        P(),
        P(None, None, "orb"),
        P(),
    )
    out_specs = (P("orb", "grid"), P("orb", "grid"))
    return jax.shard_map(body, mesh=mesh, in_specs=in_specs, out_specs=out_specs, check_vma=False)
```

```python
import functools

import jax
import jax.numpy as jnp
import numpy as np
from jax import lax
from jax.experimental import pallas as pl
from jax.experimental.pallas import tpu as pltpu
from jax.sharding import PartitionSpec as P

NX = 96
NY = 96
REACH = 6
ATOM_DEV = 4
PLANE = NX * NY
BLOCK_ROWS = 8
BLOCK = BLOCK_ROWS * NX
STEP_PLANES = 3
SLOTS = 16
TILE = 256
LANES = 128
CHUNKS = ((0, 12),)
VMEM_LIMIT = 24 * 2**20

stencil_weights = (
    -5369.0 / 1800.0,
    12.0 / 7.0,
    -15.0 / 56.0,
    10.0 / 189.0,
    -1.0 / 112.0,
    2.0 / 1925.0,
    -1.0 / 16632.0,
)
cheb_center = 6.0
cheb_half = 6.0

TAPS = {
    0: ((0, 0, 3), (1, 0, 3), (2, 0, 1)),
    1: ((0, 1, 3), (1, 0, 3), (2, 0, 2)),
    2: ((0, 2, 3), (1, 0, 3), (2, 0, 3)),
}


def plane_taps():
    cell = np.arange(BLOCK)
    row, column = cell // NX, cell % NX
    out = np.zeros((3, BLOCK, BLOCK), np.float64)
    for block in range(3):
        source_row = row + (block - 1) * BLOCK_ROWS
        jump_row = np.abs(source_row[:, None] - row[None, :])
        jump_column = np.abs(column[:, None] - column[None, :])
        for distance in range(1, REACH + 1):
            hit = ((jump_row == distance) & (jump_column == 0)) | (
                (jump_row == 0) & (jump_column == distance)
            )
            out[block][hit] = stencil_weights[distance] / stencil_weights[1]
    return out.astype(jnp.bfloat16)


def z_sum(planes, target, first):
    total = None
    for at, values in enumerate(planes):
        distance = abs(first + at - target)
        if 1 <= distance <= REACH:
            term = stencil_weights[distance] * values
            total = term if total is None else total + term
    return total


def block_diagonal(depth, rows, columns):
    row = lax.broadcasted_iota(jnp.int32, (depth * rows, depth * columns), 0) // rows
    column = lax.broadcasted_iota(jnp.int32, (depth * rows, depth * columns), 1) // columns
    return row == column


def split(values):
    high = values.astype(jnp.bfloat16)
    return high, (values - high.astype(jnp.float32)).astype(jnp.bfloat16)


def aligned(index, multiple):
    return pl.multiple_of(index, multiple)


class Sizes:
    def __init__(self, panel, cells, entries):
        self.panel, self.cells, self.entries = panel, cells, entries
        self.depth = cells // PLANE
        self.blocks = PLANE // BLOCK
        self.stride = self.depth * panel
        self.atoms = self.depth * SLOTS

    def chunk_cells(self, chunk):
        low, high = CHUNKS[chunk]
        return self.depth * (high - low) * BLOCK

    def start(self, plane, block, part=0):
        return aligned(plane * PLANE + block * BLOCK + part * TILE, LANES)

    def chunk_start(self, chunk, plane, block, part=0):
        low, high = CHUNKS[chunk]
        at = plane * (high - low) * BLOCK + (block - low) * BLOCK + part * TILE
        return aligned(at, LANES)

    def each_block(self, chunk, one):
        def step(block, carry):
            one(block)
            return carry

        lax.fori_loop(*CHUNKS[chunk], step, None, unroll=2)


def pack_planes(n, source, targets):
    zero = jnp.zeros((n.stride, BLOCK), jnp.bfloat16)
    for target in targets:
        target[0 : n.stride, :] = zero
        target[(n.blocks + 1) * n.stride : (n.blocks + 2) * n.stride, :] = zero

    def one(block, carry):
        for pair in range(n.depth // 2):
            halves = [
                source[:, pl.ds(n.start(plane, block), BLOCK)].astype(jnp.float32)
                for plane in (2 * pair, 2 * pair + 1)
            ]
            parts = split(jnp.concatenate(halves, axis=0))
            row = aligned((block + 1) * n.stride + pair * 2 * n.panel, 16)
            for target, part in zip(targets, parts):
                target[pl.ds(row, 2 * n.panel), :] = part
        return carry

    lax.fori_loop(0, n.blocks, one, None)


def apply_taps(n, packs, taps, out):
    rows = n.blocks * n.stride
    for tile, parts in TAPS.items():
        total = None
        for packed in packs:
            for block, low, high in parts:
                term = jnp.dot(
                    packed[block * n.stride : block * n.stride + rows, low * TILE : high * TILE],
                    taps[block, low * TILE : high * TILE, tile * TILE : (tile + 1) * TILE],
                    preferred_element_type=jnp.float32,
                )
                total = term if total is None else total + term
        out[:, tile * TILE : (tile + 1) * TILE] = total


def atom_partial(n, packs, table, out):
    total = None
    for block in range(n.blocks):
        weights = table[block * n.atoms : (block + 1) * n.atoms, :]
        for packed in packs:
            rows = packed[(block + 1) * n.stride : (block + 2) * n.stride, :]
            term = lax.dot_general(
                rows, weights, (((1,), (1,)), ((), ())), preferred_element_type=jnp.float32
            )
            total = term if total is None else total + term
    total = jnp.where(block_diagonal(n.depth, n.panel, SLOTS), total, 0.0)
    folded = total[0 : n.panel, :]
    for plane in range(1, n.depth):
        folded = folded + total[plane * n.panel : (plane + 1) * n.panel, :]
    wide = jnp.concatenate([folded, jnp.zeros((n.panel, LANES - n.atoms), jnp.float32)], axis=1)
    total = wide
    for plane in range(1, n.depth):
        total = total + pltpu.roll(wide, LANES - plane * SLOTS, 1)
    lane = lax.broadcasted_iota(jnp.int32, total.shape, 1)
    out[...] = jnp.where(lane < SLOTS, total, 0.0)


def near_sums(n, tables, strength):
    own, partner, far, partner_far = tables
    outward = 2 * (lax.axis_index("grid") % 2) - 1
    slab = lax.axis_index("grid")
    total = own[...]
    for table, offset in (
        (partner[...], -outward),
        (far[0 : n.panel, :], outward),
        (far[n.panel : 2 * n.panel, :], 2 * outward),
        (partner_far[0 : n.panel, :], -2 * outward),
        (partner_far[n.panel : 2 * n.panel, :], -3 * outward),
    ):
        total = total + pltpu.roll(table, (offset * ATOM_DEV + LANES) % LANES, 1)
    count = strength.shape[1]
    near = strength[...]
    if count < LANES:
        near = jnp.concatenate([near, jnp.zeros((1, LANES - count), jnp.float32)], axis=1)
    near = jnp.broadcast_to(near, total.shape)
    near = pltpu.roll(near, (ATOM_DEV - slab * ATOM_DEV + LANES) % LANES, 1)
    lane = lax.broadcasted_iota(jnp.int32, total.shape, 1)
    return jnp.where(lane < 3 * ATOM_DEV, total * near, 0.0)


def on_planes(n, sums):
    wide = sums
    for plane in range(1, n.depth):
        wide = wide + pltpu.roll(sums, plane * SLOTS, 1)
    return wide[:, 0 : n.atoms]


def by_side(inner, outer, run):
    odd = lax.axis_index("grid") % 2
    pl.when(odd == 0)(functools.partial(run, outer, inner))
    pl.when(odd == 1)(functools.partial(run, inner, outer))


def level_of(n, potential, plane, block, part):
    first = plane * (PLANE // LANES) + block * (BLOCK // LANES) + part * (TILE // LANES)
    return jnp.concatenate(
        [
            jnp.broadcast_to(potential[pl.ds(first + k, 1), :], (n.panel, LANES))
            for k in range(TILE // LANES)
        ],
        axis=1,
    )


def local_part(n, field, potential, sums, emit):
    for chunk in range(len(CHUNKS)):

        def one(block):
            for part in range(BLOCK // TILE):
                starts = [n.start(plane, block, part) for plane in range(n.depth)]
                planes = [field[:, pl.ds(start, TILE)].astype(jnp.float32) for start in starts]
                for plane in range(n.depth):
                    row = aligned(block * n.stride + plane * n.panel, 8)
                    lap = (
                        3.0 * stencil_weights[0] * planes[plane]
                        + stencil_weights[1]
                        * sums[pl.ds(row, n.panel), part * TILE : (part + 1) * TILE]
                        + z_sum(planes, plane, 0)
                    )
                    level = level_of(n, potential, plane, block, part)
                    value = -0.5 * lap + (level - cheb_center) * planes[plane]
                    emit(chunk, (plane, block, part), pl.ds(starts[plane], TILE), value)

        n.each_block(chunk, one)


def lap_beside(n, low, high, starts):
    below = [low[:, pl.ds(start, TILE)].astype(jnp.float32) for start in starts]
    above = [high[:, pl.ds(start, TILE)].astype(jnp.float32) for start in starts]
    return [
        z_sum(below, plane, -n.depth) + z_sum(above, plane, n.depth) for plane in range(n.depth)
    ]


def table_kernel(n, field, entry_ref, table, partial, packed, place):
    rows = n.entries // LANES

    def entry_row(first):
        return jnp.concatenate(
            [entry_ref[first * rows + k : first * rows + k + 1, :] for k in range(rows)], axis=1
        )

    row_at, lane_at = entry_row(0), entry_row(1)
    lane = lax.broadcasted_iota(jnp.int32, (BLOCK, n.entries), 0).astype(jnp.float32)
    place[...] = jnp.where(lane == lane_at, entry_row(2), 0.0).astype(jnp.bfloat16)
    chunk = 4 * n.atoms
    for first in range(0, n.blocks * n.atoms, chunk):
        row = lax.broadcasted_iota(jnp.int32, (chunk, n.entries), 0) + first
        hit = jnp.where(row.astype(jnp.float32) == row_at, 1.0, 0.0).astype(jnp.bfloat16)
        table[first : first + chunk, :] = lax.dot_general(
            hit, place[...], (((1,), (1,)), ((), ())), preferred_element_type=jnp.float32
        ).astype(jnp.bfloat16)
    pack_planes(n, field, (packed,))
    atom_partial(n, (packed,), table, partial)


def first_local_kernel(n, field, packed, potential, taps, out, sums):
    apply_taps(n, (packed,), taps, sums)

    def emit(chunk, tile, cells, value):
        out[:, cells] = value * (1.0 / cheb_half)

    local_part(n, field, potential, sums, emit)


def first_halo_kernel(n, local, inner, outer, table, strength, *refs):
    tables, out, sents = refs[:4], refs[4], refs[5:]
    wide = on_planes(n, near_sums(n, tables, strength))
    rows = jnp.where(
        block_diagonal(n.depth, n.panel, SLOTS), jnp.concatenate([wide] * n.depth, axis=0), 0.0
    )
    rows = jnp.concatenate(split(rows), axis=1)

    def run(low, high):
        for chunk in range(len(CHUNKS)):

            def one(block):
                weights = table[pl.ds(aligned(block * n.atoms, 16), n.atoms), :]
                weights = jnp.concatenate([weights, weights], axis=0)
                spread = jnp.dot(rows, weights, preferred_element_type=jnp.float32)
                for part in range(BLOCK // TILE):
                    starts = [n.start(plane, block, part) for plane in range(n.depth)]
                    laps = lap_beside(n, low, high, starts)
                    for plane in range(n.depth):
                        near = spread[
                            plane * n.panel : (plane + 1) * n.panel,
                            part * TILE : (part + 1) * TILE,
                        ]
                        cells = pl.ds(starts[plane], TILE)
                        value = local[:, cells] + (near - 0.5 * laps[plane]) * (1.0 / cheb_half)
                        out[:, cells] = value
                        cells = pl.ds(n.chunk_start(chunk, plane, block, part), TILE)
                        sents[chunk][:, cells] = value.astype(jnp.bfloat16)

            n.each_block(chunk, one)

    by_side(inner, outer, run)


def second_sums_kernel(n, field, table, partial, packed, rest):
    pack_planes(n, field, (packed, rest))
    atom_partial(n, (packed, rest), table, partial)


def second_local_kernel(n, field, initial, packed, rest, potential, taps, *refs):
    *outs, sums = refs
    apply_taps(n, (packed, rest), taps, sums)

    def emit(chunk, tile, cells, value):
        value = value * (2.0 / cheb_half) - initial[:, cells].astype(jnp.float32)
        outs[chunk][:, pl.ds(n.chunk_start(chunk, *tile), TILE)] = value

    local_part(n, field, potential, sums, emit)


def second_halo_kernel(n, chunk, local, inner, outer, out):
    def run(low, high):
        def one(block):
            for part in range(BLOCK // TILE):
                starts = [n.chunk_start(chunk, plane, block, part) for plane in range(n.depth)]
                laps = lap_beside(n, low, high, starts)
                for plane in range(n.depth):
                    cells = pl.ds(starts[plane], TILE)
                    value = local[:, cells] - laps[plane] * (1.0 / cheb_half)
                    out[:, cells] = value.astype(jnp.bfloat16)

        n.each_block(chunk, one)

    by_side(inner, outer, run)


def atoms_kernel(n, strength, *refs):
    *tables, out = refs
    out[...] = near_sums(n, tables, strength) * (2.0 / cheb_half)


def rotation_rows(n, shifts, owner, ritz):
    columns = ritz.shape[1]
    steps = ritz[...].astype(jnp.float32)
    blocks = []
    for shift in shifts:
        source = lax.axis_index("orb") + (lax.axis_size("orb") - shift)
        source = jnp.where(source >= lax.axis_size("orb"), source - lax.axis_size("orb"), source)
        total = jnp.zeros((n.panel, columns), jnp.float32)
        for step in range(ritz.shape[0] // n.panel):
            rows = steps[step * n.panel : (step + 1) * n.panel, :]
            total = total + jnp.where(owner[step] == source, rows, 0.0)
        blocks.append(total)
    weights = jnp.concatenate(blocks, axis=0)
    eye = lax.broadcasted_iota(jnp.int32, (columns, columns), 0) == lax.broadcasted_iota(
        jnp.int32, (columns, columns), 1
    )
    return lax.dot_general(
        eye.astype(jnp.float32),
        weights,
        (((1,), (1,)), ((), ())),
        precision=lax.Precision.HIGHEST,
        preferred_element_type=jnp.float32,
    )


def with_slots(rotation, added):
    both = jnp.dot(
        rotation,
        added[:, 0:SLOTS],
        precision=lax.Precision.HIGHEST,
        preferred_element_type=jnp.float32,
    )
    return jnp.concatenate([rotation, both], axis=1)


def twice(parts, table, n, plane, block):
    atoms = table[pl.ds(aligned(block * n.atoms + plane * SLOTS, 16), SLOTS), :]
    parts = parts + [atoms.astype(jnp.float32)]
    return jnp.concatenate(parts * 2, axis=0).astype(jnp.bfloat16)


def rotate_own_kernel(
    n, orbs, owner, ritz, added, panel, table, filtered, rotated, rest, rows_ref
):
    columns = ritz.shape[1]

    @pl.when(pl.program_id(0) == 0)
    def _():
        rotation = rotation_rows(n, range(orbs), owner, ritz)
        rest[...] = rotation[:, n.panel :]
        top = with_slots(rotation[:, 0 : n.panel], added[...])
        bottom = jnp.concatenate(
            [jnp.zeros((n.panel, n.panel), jnp.float32), added[:, 0:SLOTS]], axis=1
        )
        rows_ref[...] = jnp.concatenate(split(jnp.concatenate([top, bottom], axis=0)), axis=1)

    matrix = rows_ref[...]
    for at in range(STEP_PLANES * n.blocks):
        plane, block = pl.program_id(0) * STEP_PLANES + at // n.blocks, at % n.blocks
        own = panel[:, pl.ds(n.start(plane, block), BLOCK)].astype(jnp.float32)
        both = jnp.dot(
            matrix,
            twice([own], table, n, plane, block),
            preferred_element_type=jnp.float32,
        )
        cells = slice(at * BLOCK, (at + 1) * BLOCK)
        filtered[:, cells] = (own + both[columns : columns + n.panel, :]).astype(jnp.bfloat16)
        rotated[:, pl.ds(n.start(plane, block), BLOCK)] = both[0:columns, :]


def rotate_rest_kernel(n, count, rotation, *refs):
    *refs, own, table, rotated, rows_ref = refs
    adds, panels = refs[:count], refs[count:]

    @pl.when(pl.program_id(0) == 0)
    def _():
        added = jnp.concatenate([add[...] for add in adds], axis=0)
        rows_ref[...] = jnp.concatenate(split(with_slots(rotation[...], added)), axis=1)

    matrix = rows_ref[...]
    for at in range(STEP_PLANES * n.blocks):
        plane, block = pl.program_id(0) * STEP_PLANES + at // n.blocks, at % n.blocks
        cells = pl.ds(n.start(plane, block), BLOCK)
        parts = [p[:, at * BLOCK : (at + 1) * BLOCK].astype(jnp.float32) for p in panels]
        total = own[:, cells] + jnp.dot(
            matrix,
            twice(parts, table, n, plane, block),
            preferred_element_type=jnp.float32,
        )
        rotated[:, at * BLOCK : (at + 1) * BLOCK] = total.astype(jnp.bfloat16)


def call(kernel, out_shape, scratch, flops, *operands):
    bytes_accessed = sum(int(np.prod(o.shape)) * o.dtype.itemsize for o in operands)
    return pl.pallas_call(
        kernel,
        out_shape=out_shape,
        in_specs=[pl.BlockSpec(memory_space=pltpu.VMEM)] * len(operands),
        out_specs=jax.tree.map(lambda _: pl.BlockSpec(memory_space=pltpu.VMEM), out_shape),
        scratch_shapes=scratch,
        compiler_params=pltpu.CompilerParams(vmem_limit_bytes=VMEM_LIMIT),
        cost_estimate=pl.CostEstimate(
            flops=flops, bytes_accessed=bytes_accessed, transcendentals=0
        ),
    )(*operands)


def swapped(block, partner):
    count = lax.axis_size("grid")
    pairs = [(i, partner(i)) for i in range(count) if 0 <= partner(i) < count]
    return lax.ppermute(block, "grid", pairs)


def core_partner(i):
    return i ^ 1


def outer_partner(i):
    return i + 1 if i % 2 else i - 1


def exchange_sums(partial, after=None):
    partner = swapped(partial, core_partner)
    both = jnp.concatenate([partial, partner], axis=0)
    if after is not None:
        both, _ = lax.optimization_barrier((both, after))
    far = swapped(both, outer_partner)
    return partial, partner, far, swapped(far, core_partner)


def body(
    orbitals,
    potential,
    projector_atom,
    projector_cell,
    projector_value,
    atom_strength,
    ritz_rotation,
    panel_owner,
):
    panel, cells = orbitals.shape
    n = Sizes(panel, cells, projector_atom.shape[0])
    chunks = range(len(CHUNKS))
    taps = jnp.asarray(plane_taps())
    level = potential.reshape(n.cells // LANES, LANES)
    strength = atom_strength[None, :]

    bf16, f32 = jnp.bfloat16, jnp.float32
    shape = jax.ShapeDtypeStruct
    field = shape((panel, cells), f32)
    fields = [shape((panel, n.chunk_cells(chunk)), f32) for chunk in chunks]
    narrows = [shape((panel, n.chunk_cells(chunk)), bf16) for chunk in chunks]
    sums = shape((panel, LANES), f32)
    packed_shape = shape(((n.blocks + 2) * n.stride, BLOCK), bf16)
    tap_sums = pltpu.VMEM((n.blocks * n.stride, BLOCK), f32)

    outer = swapped(orbitals, outer_partner)
    inner = swapped(orbitals, core_partner)
    plane, inside = projector_cell // PLANE, projector_cell % PLANE
    slot = projector_atom - (lax.axis_index("grid") - 1) * ATOM_DEV
    row_at = ((inside // BLOCK) * n.depth + plane) * SLOTS + slot
    entries = jnp.concatenate(
        [
            entry.astype(f32).reshape(n.entries // LANES, LANES)
            for entry in (row_at, inside % BLOCK, projector_value)
        ],
        axis=0,
    )
    table, partial, packed = call(
        functools.partial(table_kernel, n),
        (shape((n.blocks * n.atoms, BLOCK), bf16), sums, packed_shape),
        [pltpu.VMEM((BLOCK, n.entries), bf16)],
        4 * 10**9,
        orbitals, entries,
    )
    local = call(
        functools.partial(first_local_kernel, n), field, [tap_sums], 2 * 10**9,
        orbitals, packed, level, taps,
    )
    near = exchange_sums(partial, local)
    step_field, *sents = call(
        functools.partial(first_halo_kernel, n),
        [field] + narrows, [], 10**9,
        local, inner, outer, table, strength, *near,
    )
    outers = [swapped(sent, outer_partner) for sent in sents]
    halos = [(swapped(sent, core_partner), outer) for sent, outer in zip(sents, outers)]
    partial, packed, rest = call(
        functools.partial(second_sums_kernel, n),
        (sums, packed_shape, packed_shape), [], 10**9,
        step_field, table,
    )
    locals_ = call(
        functools.partial(second_local_kernel, n), fields, [tap_sums], 3 * 10**9,
        step_field, orbitals, packed, rest, level, taps,
    )

    orb_count = lax.axis_size("orb")

    def all_orbs(block):
        return [block] + [
            lax.ppermute(block, "orb", [(i, (i + k) % orb_count) for i in range(orb_count)])
            for k in range(1, orb_count)
        ]

    near = exchange_sums(partial)
    held, _ = lax.optimization_barrier((locals_[0], near[2]))
    share = call(
        functools.partial(second_halo_kernel, n, 0), narrows[0], [], 10**9,
        held, *halos[0],
    )
    panels = all_orbs(share)
    added = call(functools.partial(atoms_kernel, n), sums, [], 10**6, strength, *near)
    adds = all_orbs(added)
    columns = ritz_rotation.shape[2]
    ritz = ritz_rotation.reshape(-1, columns)
    smem = pl.BlockSpec(memory_space=pltpu.SMEM)
    vmem = pl.BlockSpec(memory_space=pltpu.VMEM)
    planes_of = lambda rows: pl.BlockSpec((rows, STEP_PLANES * PLANE), lambda i: (0, i))
    params = pltpu.CompilerParams(vmem_limit_bytes=VMEM_LIMIT)
    rest = orb_count - 1
    filtered, rotated, rotation = pl.pallas_call(
        functools.partial(rotate_own_kernel, n, orb_count),
        grid=(n.depth // STEP_PLANES,),
        out_shape=(
            shape((panel, n.cells), bf16),
            shape((columns, n.cells), f32),
            shape((columns, rest * panel), f32),
        ),
        in_specs=[smem] + [vmem] * 4,
        out_specs=(planes_of(panel), vmem, vmem),
        scratch_shapes=[pltpu.VMEM((columns + panel, 2 * (panel + SLOTS)), bf16)],
        compiler_params=params,
    )(panel_owner, ritz, adds[0], share, table)
    rotated = pl.pallas_call(
        functools.partial(rotate_rest_kernel, n, rest),
        grid=(n.depth // STEP_PLANES,),
        out_shape=shape((columns, n.cells), bf16),
        in_specs=[vmem] * (1 + rest) + [planes_of(panel)] * rest + [vmem] * 2,
        out_specs=planes_of(columns),
        scratch_shapes=[pltpu.VMEM((columns, 2 * (rest * panel + SLOTS)), bf16)],
        compiler_params=params,
    )(rotation, *adds[1:], *panels[1:], rotated, table)
    return (filtered, rotated)


def solution(mesh):
    in_specs = (
        P("orb", "grid"),
        P("grid"),
        P("grid"),
        P("grid"),
        P("grid"),
        P(),
        P(None, None, "orb"),
        P(),
    )
    out_specs = (P("orb", "grid"), P("orb", "grid"))
    return jax.shard_map(body, mesh=mesh, in_specs=in_specs, out_specs=out_specs, check_vma=False)
```

```python
import functools

import jax
import jax.numpy as jnp
import numpy as np
from jax import lax
from jax.experimental import pallas as pl
from jax.experimental.pallas import tpu as pltpu
from jax.sharding import PartitionSpec as P

NX = 96
NY = 96
REACH = 6
ATOM_DEV = 4
PLANE = NX * NY
BLOCK_ROWS = 8
BLOCK = BLOCK_ROWS * NX
STEP_PLANES = 3
SLOTS = 16
TILE = 256
LANES = 128
CHUNKS = ((0, 12),)
VMEM_LIMIT = 24 * 2**20

stencil_weights = (
    -5369.0 / 1800.0,
    12.0 / 7.0,
    -15.0 / 56.0,
    10.0 / 189.0,
    -1.0 / 112.0,
    2.0 / 1925.0,
    -1.0 / 16632.0,
)
cheb_center = 6.0
cheb_half = 6.0

TAPS = {
    0: ((0, 0, 3), (1, 0, 3), (2, 0, 1)),
    1: ((0, 1, 3), (1, 0, 3), (2, 0, 2)),
    2: ((0, 2, 3), (1, 0, 3), (2, 0, 3)),
}


def plane_taps():
    cell = np.arange(BLOCK)
    row, column = cell // NX, cell % NX
    out = np.zeros((3, BLOCK, BLOCK), np.float64)
    for block in range(3):
        source_row = row + (block - 1) * BLOCK_ROWS
        jump_row = np.abs(source_row[:, None] - row[None, :])
        jump_column = np.abs(column[:, None] - column[None, :])
        for distance in range(1, REACH + 1):
            hit = ((jump_row == distance) & (jump_column == 0)) | (
                (jump_row == 0) & (jump_column == distance)
            )
            out[block][hit] = stencil_weights[distance] / stencil_weights[1]
    return out.astype(jnp.bfloat16)


def z_sum(planes, target, first):
    total = None
    for at, values in enumerate(planes):
        distance = abs(first + at - target)
        if 1 <= distance <= REACH:
            term = stencil_weights[distance] * values
            total = term if total is None else total + term
    return total


def block_diagonal(depth, rows, columns):
    row = lax.broadcasted_iota(jnp.int32, (depth * rows, depth * columns), 0) // rows
    column = lax.broadcasted_iota(jnp.int32, (depth * rows, depth * columns), 1) // columns
    return row == column


def split(values):
    high = values.astype(jnp.bfloat16)
    return high, (values - high.astype(jnp.float32)).astype(jnp.bfloat16)


def aligned(index, multiple):
    return pl.multiple_of(index, multiple)


class Sizes:
    def __init__(self, panel, cells, entries):
        self.panel, self.cells, self.entries = panel, cells, entries
        self.depth = cells // PLANE
        self.blocks = PLANE // BLOCK
        self.stride = self.depth * panel
        self.atoms = self.depth * SLOTS

    def chunk_cells(self, chunk):
        low, high = CHUNKS[chunk]
        return self.depth * (high - low) * BLOCK

    def start(self, plane, block, part=0):
        return aligned(plane * PLANE + block * BLOCK + part * TILE, LANES)

    def chunk_start(self, chunk, plane, block, part=0):
        low, high = CHUNKS[chunk]
        at = plane * (high - low) * BLOCK + (block - low) * BLOCK + part * TILE
        return aligned(at, LANES)

    def each_block(self, chunk, one):
        def step(block, carry):
            one(block)
            return carry

        lax.fori_loop(*CHUNKS[chunk], step, None, unroll=4)


def pack_planes(n, source, targets):
    zero = jnp.zeros((n.stride, BLOCK), jnp.bfloat16)
    for target in targets:
        target[0 : n.stride, :] = zero
        target[(n.blocks + 1) * n.stride : (n.blocks + 2) * n.stride, :] = zero

    def one(block, carry):
        for pair in range(n.depth // 2):
            halves = [
                source[:, pl.ds(n.start(plane, block), BLOCK)].astype(jnp.float32)
                for plane in (2 * pair, 2 * pair + 1)
            ]
            parts = split(jnp.concatenate(halves, axis=0))
            row = aligned((block + 1) * n.stride + pair * 2 * n.panel, 16)
            for target, part in zip(targets, parts):
                target[pl.ds(row, 2 * n.panel), :] = part
        return carry

    lax.fori_loop(0, n.blocks, one, None)


def apply_taps(n, packs, taps, out):
    rows = n.blocks * n.stride
    for tile, parts in TAPS.items():
        total = None
        for packed in packs:
            for block, low, high in parts:
                term = jnp.dot(
                    packed[block * n.stride : block * n.stride + rows, low * TILE : high * TILE],
                    taps[block, low * TILE : high * TILE, tile * TILE : (tile + 1) * TILE],
                    preferred_element_type=jnp.float32,
                )
                total = term if total is None else total + term
        out[:, tile * TILE : (tile + 1) * TILE] = total


def atom_partial(n, packs, table, out):
    total = None
    for block in range(n.blocks):
        weights = table[block * n.atoms : (block + 1) * n.atoms, :]
        for packed in packs:
            rows = packed[(block + 1) * n.stride : (block + 2) * n.stride, :]
            term = lax.dot_general(
                rows, weights, (((1,), (1,)), ((), ())), preferred_element_type=jnp.float32
            )
            total = term if total is None else total + term
    total = jnp.where(block_diagonal(n.depth, n.panel, SLOTS), total, 0.0)
    folded = total[0 : n.panel, :]
    for plane in range(1, n.depth):
        folded = folded + total[plane * n.panel : (plane + 1) * n.panel, :]
    wide = jnp.concatenate([folded, jnp.zeros((n.panel, LANES - n.atoms), jnp.float32)], axis=1)
    total = wide
    for plane in range(1, n.depth):
        total = total + pltpu.roll(wide, LANES - plane * SLOTS, 1)
    lane = lax.broadcasted_iota(jnp.int32, total.shape, 1)
    out[...] = jnp.where(lane < SLOTS, total, 0.0)


def near_sums(n, tables, strength):
    own, partner, far, partner_far = tables
    outward = 2 * (lax.axis_index("grid") % 2) - 1
    slab = lax.axis_index("grid")
    total = own[...]
    for table, offset in (
        (partner[...], -outward),
        (far[0 : n.panel, :], outward),
        (far[n.panel : 2 * n.panel, :], 2 * outward),
        (partner_far[0 : n.panel, :], -2 * outward),
        (partner_far[n.panel : 2 * n.panel, :], -3 * outward),
    ):
        total = total + pltpu.roll(table, (offset * ATOM_DEV + LANES) % LANES, 1)
    count = strength.shape[1]
    near = strength[...]
    if count < LANES:
        near = jnp.concatenate([near, jnp.zeros((1, LANES - count), jnp.float32)], axis=1)
    near = jnp.broadcast_to(near, total.shape)
    near = pltpu.roll(near, (ATOM_DEV - slab * ATOM_DEV + LANES) % LANES, 1)
    lane = lax.broadcasted_iota(jnp.int32, total.shape, 1)
    return jnp.where(lane < 3 * ATOM_DEV, total * near, 0.0)


def on_planes(n, sums):
    wide = sums
    for plane in range(1, n.depth):
        wide = wide + pltpu.roll(sums, plane * SLOTS, 1)
    return wide[:, 0 : n.atoms]


def by_side(inner, outer, run):
    odd = lax.axis_index("grid") % 2
    pl.when(odd == 0)(functools.partial(run, outer, inner))
    pl.when(odd == 1)(functools.partial(run, inner, outer))


def level_of(n, potential, plane, block, part):
    first = plane * (PLANE // LANES) + block * (BLOCK // LANES) + part * (TILE // LANES)
    return jnp.concatenate(
        [
            jnp.broadcast_to(potential[pl.ds(first + k, 1), :], (n.panel, LANES))
            for k in range(TILE // LANES)
        ],
        axis=1,
    )


def local_part(n, field, potential, sums, emit):
    for chunk in range(len(CHUNKS)):

        def one(block):
            for part in range(BLOCK // TILE):
                starts = [n.start(plane, block, part) for plane in range(n.depth)]
                planes = [field[:, pl.ds(start, TILE)].astype(jnp.float32) for start in starts]
                for plane in range(n.depth):
                    row = aligned(block * n.stride + plane * n.panel, 8)
                    lap = (
                        3.0 * stencil_weights[0] * planes[plane]
                        + stencil_weights[1]
                        * sums[pl.ds(row, n.panel), part * TILE : (part + 1) * TILE]
                        + z_sum(planes, plane, 0)
                    )
                    level = level_of(n, potential, plane, block, part)
                    value = -0.5 * lap + (level - cheb_center) * planes[plane]
                    emit(chunk, (plane, block, part), pl.ds(starts[plane], TILE), value)

        n.each_block(chunk, one)


def lap_beside(n, low, high, starts):
    below = [low[:, pl.ds(start, TILE)].astype(jnp.float32) for start in starts]
    above = [high[:, pl.ds(start, TILE)].astype(jnp.float32) for start in starts]
    return [
        z_sum(below, plane, -n.depth) + z_sum(above, plane, n.depth) for plane in range(n.depth)
    ]


def table_kernel(n, field, entry_ref, table, partial, packed, place):
    rows = n.entries // LANES

    def entry_row(first):
        return jnp.concatenate(
            [entry_ref[first * rows + k : first * rows + k + 1, :] for k in range(rows)], axis=1
        )

    row_at, lane_at = entry_row(0), entry_row(1)
    lane = lax.broadcasted_iota(jnp.int32, (BLOCK, n.entries), 0).astype(jnp.float32)
    place[...] = jnp.where(lane == lane_at, entry_row(2), 0.0).astype(jnp.bfloat16)
    chunk = 4 * n.atoms
    for first in range(0, n.blocks * n.atoms, chunk):
        row = lax.broadcasted_iota(jnp.int32, (chunk, n.entries), 0) + first
        hit = jnp.where(row.astype(jnp.float32) == row_at, 1.0, 0.0).astype(jnp.bfloat16)
        table[first : first + chunk, :] = lax.dot_general(
            hit, place[...], (((1,), (1,)), ((), ())), preferred_element_type=jnp.float32
        ).astype(jnp.bfloat16)
    pack_planes(n, field, (packed,))
    atom_partial(n, (packed,), table, partial)


def first_local_kernel(n, field, packed, potential, taps, out, sums):
    apply_taps(n, (packed,), taps, sums)

    def emit(chunk, tile, cells, value):
        out[:, cells] = value * (1.0 / cheb_half)

    local_part(n, field, potential, sums, emit)


def first_halo_kernel(n, local, inner, outer, table, strength, *refs):
    tables, out, sents = refs[:4], refs[4], refs[5:]
    wide = on_planes(n, near_sums(n, tables, strength))
    rows = jnp.where(
        block_diagonal(n.depth, n.panel, SLOTS), jnp.concatenate([wide] * n.depth, axis=0), 0.0
    )
    rows = jnp.concatenate(split(rows), axis=1)

    def run(low, high):
        for chunk in range(len(CHUNKS)):

            def one(block):
                weights = table[pl.ds(aligned(block * n.atoms, 16), n.atoms), :]
                weights = jnp.concatenate([weights, weights], axis=0)
                spread = jnp.dot(rows, weights, preferred_element_type=jnp.float32)
                for part in range(BLOCK // TILE):
                    starts = [n.start(plane, block, part) for plane in range(n.depth)]
                    laps = lap_beside(n, low, high, starts)
                    for plane in range(n.depth):
                        near = spread[
                            plane * n.panel : (plane + 1) * n.panel,
                            part * TILE : (part + 1) * TILE,
                        ]
                        cells = pl.ds(starts[plane], TILE)
                        value = local[:, cells] + (near - 0.5 * laps[plane]) * (1.0 / cheb_half)
                        out[:, cells] = value
                        cells = pl.ds(n.chunk_start(chunk, plane, block, part), TILE)
                        sents[chunk][:, cells] = value.astype(jnp.bfloat16)

            n.each_block(chunk, one)

    by_side(inner, outer, run)


def second_sums_kernel(n, field, table, partial, packed, rest):
    pack_planes(n, field, (packed, rest))
    atom_partial(n, (packed, rest), table, partial)


def second_local_kernel(n, field, initial, packed, rest, potential, taps, *refs):
    *outs, sums = refs
    apply_taps(n, (packed, rest), taps, sums)

    def emit(chunk, tile, cells, value):
        value = value * (2.0 / cheb_half) - initial[:, cells].astype(jnp.float32)
        outs[chunk][:, pl.ds(n.chunk_start(chunk, *tile), TILE)] = value

    local_part(n, field, potential, sums, emit)


def second_halo_kernel(n, chunk, local, inner, outer, out):
    def run(low, high):
        def one(block):
            for part in range(BLOCK // TILE):
                starts = [n.chunk_start(chunk, plane, block, part) for plane in range(n.depth)]
                laps = lap_beside(n, low, high, starts)
                for plane in range(n.depth):
                    cells = pl.ds(starts[plane], TILE)
                    value = local[:, cells] - laps[plane] * (1.0 / cheb_half)
                    out[:, cells] = value.astype(jnp.bfloat16)

        n.each_block(chunk, one)

    by_side(inner, outer, run)


def atoms_kernel(n, strength, *refs):
    *tables, out = refs
    out[...] = near_sums(n, tables, strength) * (2.0 / cheb_half)


def rotation_rows(n, shifts, owner, ritz):
    columns = ritz.shape[1]
    steps = ritz[...].astype(jnp.float32)
    blocks = []
    for shift in shifts:
        source = lax.axis_index("orb") + (lax.axis_size("orb") - shift)
        source = jnp.where(source >= lax.axis_size("orb"), source - lax.axis_size("orb"), source)
        total = jnp.zeros((n.panel, columns), jnp.float32)
        for step in range(ritz.shape[0] // n.panel):
            rows = steps[step * n.panel : (step + 1) * n.panel, :]
            total = total + jnp.where(owner[step] == source, rows, 0.0)
        blocks.append(total)
    weights = jnp.concatenate(blocks, axis=0)
    eye = lax.broadcasted_iota(jnp.int32, (columns, columns), 0) == lax.broadcasted_iota(
        jnp.int32, (columns, columns), 1
    )
    return lax.dot_general(
        eye.astype(jnp.float32),
        weights,
        (((1,), (1,)), ((), ())),
        precision=lax.Precision.HIGHEST,
        preferred_element_type=jnp.float32,
    )


def with_slots(rotation, added):
    both = jnp.dot(
        rotation,
        added[:, 0:SLOTS],
        precision=lax.Precision.HIGHEST,
        preferred_element_type=jnp.float32,
    )
    return jnp.concatenate([rotation, both], axis=1)


def twice(parts, table, n, plane, block):
    atoms = table[pl.ds(aligned(block * n.atoms + plane * SLOTS, 16), SLOTS), :]
    parts = parts + [atoms.astype(jnp.float32)]
    return jnp.concatenate(parts * 2, axis=0).astype(jnp.bfloat16)


def rotate_own_kernel(
    n, orbs, owner, ritz, added, panel, table, filtered, rotated, rest, rows_ref
):
    columns = ritz.shape[1]

    @pl.when(pl.program_id(0) == 0)
    def _():
        rotation = rotation_rows(n, range(orbs), owner, ritz)
        rest[...] = rotation[:, n.panel :]
        top = with_slots(rotation[:, 0 : n.panel], added[...])
        bottom = jnp.concatenate(
            [jnp.zeros((n.panel, n.panel), jnp.float32), added[:, 0:SLOTS]], axis=1
        )
        rows_ref[...] = jnp.concatenate(split(jnp.concatenate([top, bottom], axis=0)), axis=1)

    matrix = rows_ref[...]
    for at in range(STEP_PLANES * n.blocks):
        plane, block = pl.program_id(0) * STEP_PLANES + at // n.blocks, at % n.blocks
        own = panel[:, pl.ds(n.start(plane, block), BLOCK)].astype(jnp.float32)
        both = jnp.dot(
            matrix,
            twice([own], table, n, plane, block),
            preferred_element_type=jnp.float32,
        )
        cells = slice(at * BLOCK, (at + 1) * BLOCK)
        filtered[:, cells] = (own + both[columns : columns + n.panel, :]).astype(jnp.bfloat16)
        rotated[:, pl.ds(n.start(plane, block), BLOCK)] = both[0:columns, :]


def rotate_rest_kernel(n, count, rotation, *refs):
    *refs, own, table, rotated, rows_ref = refs
    adds, panels = refs[:count], refs[count:]

    @pl.when(pl.program_id(0) == 0)
    def _():
        added = jnp.concatenate([add[...] for add in adds], axis=0)
        rows_ref[...] = jnp.concatenate(split(with_slots(rotation[...], added)), axis=1)

    matrix = rows_ref[...]
    for at in range(STEP_PLANES * n.blocks):
        plane, block = pl.program_id(0) * STEP_PLANES + at // n.blocks, at % n.blocks
        cells = pl.ds(n.start(plane, block), BLOCK)
        parts = [p[:, at * BLOCK : (at + 1) * BLOCK].astype(jnp.float32) for p in panels]
        total = own[:, cells] + jnp.dot(
            matrix,
            twice(parts, table, n, plane, block),
            preferred_element_type=jnp.float32,
        )
        rotated[:, at * BLOCK : (at + 1) * BLOCK] = total.astype(jnp.bfloat16)


def call(kernel, out_shape, scratch, flops, *operands):
    bytes_accessed = sum(int(np.prod(o.shape)) * o.dtype.itemsize for o in operands)
    return pl.pallas_call(
        kernel,
        out_shape=out_shape,
        in_specs=[pl.BlockSpec(memory_space=pltpu.VMEM)] * len(operands),
        out_specs=jax.tree.map(lambda _: pl.BlockSpec(memory_space=pltpu.VMEM), out_shape),
        scratch_shapes=scratch,
        compiler_params=pltpu.CompilerParams(vmem_limit_bytes=VMEM_LIMIT),
        cost_estimate=pl.CostEstimate(
            flops=flops, bytes_accessed=bytes_accessed, transcendentals=0
        ),
    )(*operands)


def swapped(block, partner):
    count = lax.axis_size("grid")
    pairs = [(i, partner(i)) for i in range(count) if 0 <= partner(i) < count]
    return lax.ppermute(block, "grid", pairs)


def core_partner(i):
    return i ^ 1


def outer_partner(i):
    return i + 1 if i % 2 else i - 1


def exchange_sums(partial, after=None):
    partner = swapped(partial, core_partner)
    both = jnp.concatenate([partial, partner], axis=0)
    if after is not None:
        both, _ = lax.optimization_barrier((both, after))
    far = swapped(both, outer_partner)
    return partial, partner, far, swapped(far, core_partner)


def body(
    orbitals,
    potential,
    projector_atom,
    projector_cell,
    projector_value,
    atom_strength,
    ritz_rotation,
    panel_owner,
):
    panel, cells = orbitals.shape
    n = Sizes(panel, cells, projector_atom.shape[0])
    chunks = range(len(CHUNKS))
    taps = jnp.asarray(plane_taps())
    level = potential.reshape(n.cells // LANES, LANES)
    strength = atom_strength[None, :]

    bf16, f32 = jnp.bfloat16, jnp.float32
    shape = jax.ShapeDtypeStruct
    field = shape((panel, cells), f32)
    fields = [shape((panel, n.chunk_cells(chunk)), f32) for chunk in chunks]
    narrows = [shape((panel, n.chunk_cells(chunk)), bf16) for chunk in chunks]
    sums = shape((panel, LANES), f32)
    packed_shape = shape(((n.blocks + 2) * n.stride, BLOCK), bf16)
    tap_sums = pltpu.VMEM((n.blocks * n.stride, BLOCK), f32)

    outer = swapped(orbitals, outer_partner)
    inner = swapped(orbitals, core_partner)
    plane, inside = projector_cell // PLANE, projector_cell % PLANE
    slot = projector_atom - (lax.axis_index("grid") - 1) * ATOM_DEV
    row_at = ((inside // BLOCK) * n.depth + plane) * SLOTS + slot
    entries = jnp.concatenate(
        [
            entry.astype(f32).reshape(n.entries // LANES, LANES)
            for entry in (row_at, inside % BLOCK, projector_value)
        ],
        axis=0,
    )
    table, partial, packed = call(
        functools.partial(table_kernel, n),
        (shape((n.blocks * n.atoms, BLOCK), bf16), sums, packed_shape),
        [pltpu.VMEM((BLOCK, n.entries), bf16)],
        4 * 10**9,
        orbitals, entries,
    )
    local = call(
        functools.partial(first_local_kernel, n), field, [tap_sums], 2 * 10**9,
        orbitals, packed, level, taps,
    )
    near = exchange_sums(partial, local)
    step_field, *sents = call(
        functools.partial(first_halo_kernel, n),
        [field] + narrows, [], 10**9,
        local, inner, outer, table, strength, *near,
    )
    outers = [swapped(sent, outer_partner) for sent in sents]
    halos = [(swapped(sent, core_partner), outer) for sent, outer in zip(sents, outers)]
    partial, packed, rest = call(
        functools.partial(second_sums_kernel, n),
        (sums, packed_shape, packed_shape), [], 10**9,
        step_field, table,
    )
    locals_ = call(
        functools.partial(second_local_kernel, n), fields, [tap_sums], 3 * 10**9,
        step_field, orbitals, packed, rest, level, taps,
    )

    orb_count = lax.axis_size("orb")

    def all_orbs(block):
        return [block] + [
            lax.ppermute(block, "orb", [(i, (i + k) % orb_count) for i in range(orb_count)])
            for k in range(1, orb_count)
        ]

    near = exchange_sums(partial)
    held, _ = lax.optimization_barrier((locals_[0], near[2]))
    share = call(
        functools.partial(second_halo_kernel, n, 0), narrows[0], [], 10**9,
        held, *halos[0],
    )
    panels = all_orbs(share)
    added = call(functools.partial(atoms_kernel, n), sums, [], 10**6, strength, *near)
    adds = all_orbs(added)
    columns = ritz_rotation.shape[2]
    ritz = ritz_rotation.reshape(-1, columns)
    smem = pl.BlockSpec(memory_space=pltpu.SMEM)
    vmem = pl.BlockSpec(memory_space=pltpu.VMEM)
    planes_of = lambda rows: pl.BlockSpec((rows, STEP_PLANES * PLANE), lambda i: (0, i))
    params = pltpu.CompilerParams(vmem_limit_bytes=VMEM_LIMIT)
    rest = orb_count - 1
    filtered, rotated, rotation = pl.pallas_call(
        functools.partial(rotate_own_kernel, n, orb_count),
        grid=(n.depth // STEP_PLANES,),
        out_shape=(
            shape((panel, n.cells), bf16),
            shape((columns, n.cells), f32),
            shape((columns, rest * panel), f32),
        ),
        in_specs=[smem] + [vmem] * 4,
        out_specs=(planes_of(panel), vmem, vmem),
        scratch_shapes=[pltpu.VMEM((columns + panel, 2 * (panel + SLOTS)), bf16)],
        compiler_params=params,
    )(panel_owner, ritz, adds[0], share, table)
    rotated = pl.pallas_call(
        functools.partial(rotate_rest_kernel, n, rest),
        grid=(n.depth // STEP_PLANES,),
        out_shape=shape((columns, n.cells), bf16),
        in_specs=[vmem] * (1 + rest) + [planes_of(panel)] * rest + [vmem] * 2,
        out_specs=planes_of(columns),
        scratch_shapes=[pltpu.VMEM((columns, 2 * (rest * panel + SLOTS)), bf16)],
        compiler_params=params,
    )(rotation, *adds[1:], *panels[1:], rotated, table)
    return (filtered, rotated)


def solution(mesh):
    in_specs = (
        P("orb", "grid"),
        P("grid"),
        P("grid"),
        P("grid"),
        P("grid"),
        P(),
        P(None, None, "orb"),
        P(),
    )
    out_specs = (P("orb", "grid"), P("orb", "grid"))
    return jax.shard_map(body, mesh=mesh, in_specs=in_specs, out_specs=out_specs, check_vma=False)
```

```python
import functools

import jax
import jax.numpy as jnp
import numpy as np
from jax import lax
from jax.experimental import pallas as pl
from jax.experimental.pallas import tpu as pltpu
from jax.sharding import PartitionSpec as P

NX = 96
NY = 96
REACH = 6
ATOM_DEV = 4
PLANE = NX * NY
BLOCK_ROWS = 8
BLOCK = BLOCK_ROWS * NX
STEP_PLANES = 3
SLOTS = 16
TILE = 256
LANES = 128
CHUNKS = ((0, 12),)
VMEM_LIMIT = 24 * 2**20

stencil_weights = (
    -5369.0 / 1800.0,
    12.0 / 7.0,
    -15.0 / 56.0,
    10.0 / 189.0,
    -1.0 / 112.0,
    2.0 / 1925.0,
    -1.0 / 16632.0,
)
cheb_center = 6.0
cheb_half = 6.0

TAPS = {
    0: ((0, 0, 3), (1, 0, 3), (2, 0, 1)),
    1: ((0, 1, 3), (1, 0, 3), (2, 0, 2)),
    2: ((0, 2, 3), (1, 0, 3), (2, 0, 3)),
}


def plane_taps():
    cell = np.arange(BLOCK)
    row, column = cell // NX, cell % NX
    out = np.zeros((3, BLOCK, BLOCK), np.float64)
    for block in range(3):
        source_row = row + (block - 1) * BLOCK_ROWS
        jump_row = np.abs(source_row[:, None] - row[None, :])
        jump_column = np.abs(column[:, None] - column[None, :])
        for distance in range(1, REACH + 1):
            hit = ((jump_row == distance) & (jump_column == 0)) | (
                (jump_row == 0) & (jump_column == distance)
            )
            out[block][hit] = stencil_weights[distance] / stencil_weights[1]
    return out.astype(jnp.bfloat16)


def z_sum(planes, target, first):
    total = None
    for at, values in enumerate(planes):
        distance = abs(first + at - target)
        if 1 <= distance <= REACH:
            term = stencil_weights[distance] * values
            total = term if total is None else total + term
    return total


def block_diagonal(depth, rows, columns):
    row = lax.broadcasted_iota(jnp.int32, (depth * rows, depth * columns), 0) // rows
    column = lax.broadcasted_iota(jnp.int32, (depth * rows, depth * columns), 1) // columns
    return row == column


def split(values):
    high = values.astype(jnp.bfloat16)
    return high, (values - high.astype(jnp.float32)).astype(jnp.bfloat16)


def aligned(index, multiple):
    return pl.multiple_of(index, multiple)


class Sizes:
    def __init__(self, panel, cells, entries):
        self.panel, self.cells, self.entries = panel, cells, entries
        self.depth = cells // PLANE
        self.blocks = PLANE // BLOCK
        self.stride = self.depth * panel
        self.atoms = self.depth * SLOTS

    def chunk_cells(self, chunk):
        low, high = CHUNKS[chunk]
        return self.depth * (high - low) * BLOCK

    def start(self, plane, block, part=0):
        return aligned(plane * PLANE + block * BLOCK + part * TILE, LANES)

    def chunk_start(self, chunk, plane, block, part=0):
        low, high = CHUNKS[chunk]
        at = plane * (high - low) * BLOCK + (block - low) * BLOCK + part * TILE
        return aligned(at, LANES)

    def each_block(self, chunk, one):
        def step(block, carry):
            one(block)
            return carry

        lax.fori_loop(*CHUNKS[chunk], step, None, unroll=4)


def pack_planes(n, source, targets):
    zero = jnp.zeros((n.stride, BLOCK), jnp.bfloat16)
    for target in targets:
        target[0 : n.stride, :] = zero
        target[(n.blocks + 1) * n.stride : (n.blocks + 2) * n.stride, :] = zero

    def one(block, carry):
        for pair in range(n.depth // 2):
            halves = [
                source[:, pl.ds(n.start(plane, block), BLOCK)].astype(jnp.float32)
                for plane in (2 * pair, 2 * pair + 1)
            ]
            parts = split(jnp.concatenate(halves, axis=0))
            row = aligned((block + 1) * n.stride + pair * 2 * n.panel, 16)
            for target, part in zip(targets, parts):
                target[pl.ds(row, 2 * n.panel), :] = part
        return carry

    lax.fori_loop(0, n.blocks, one, None, unroll=4)


def apply_taps(n, packs, taps, out):
    rows = n.blocks * n.stride
    for tile, parts in TAPS.items():
        total = None
        for packed in packs:
            for block, low, high in parts:
                term = jnp.dot(
                    packed[block * n.stride : block * n.stride + rows, low * TILE : high * TILE],
                    taps[block, low * TILE : high * TILE, tile * TILE : (tile + 1) * TILE],
                    preferred_element_type=jnp.float32,
                )
                total = term if total is None else total + term
        out[:, tile * TILE : (tile + 1) * TILE] = total


def atom_partial(n, packs, table, out):
    total = None
    for block in range(n.blocks):
        weights = table[block * n.atoms : (block + 1) * n.atoms, :]
        for packed in packs:
            rows = packed[(block + 1) * n.stride : (block + 2) * n.stride, :]
            term = lax.dot_general(
                rows, weights, (((1,), (1,)), ((), ())), preferred_element_type=jnp.float32
            )
            total = term if total is None else total + term
    total = jnp.where(block_diagonal(n.depth, n.panel, SLOTS), total, 0.0)
    folded = total[0 : n.panel, :]
    for plane in range(1, n.depth):
        folded = folded + total[plane * n.panel : (plane + 1) * n.panel, :]
    wide = jnp.concatenate([folded, jnp.zeros((n.panel, LANES - n.atoms), jnp.float32)], axis=1)
    total = wide
    for plane in range(1, n.depth):
        total = total + pltpu.roll(wide, LANES - plane * SLOTS, 1)
    lane = lax.broadcasted_iota(jnp.int32, total.shape, 1)
    out[...] = jnp.where(lane < SLOTS, total, 0.0)


def near_sums(n, tables, strength):
    own, partner, far, partner_far = tables
    outward = 2 * (lax.axis_index("grid") % 2) - 1
    slab = lax.axis_index("grid")
    total = own[...]
    for table, offset in (
        (partner[...], -outward),
        (far[0 : n.panel, :], outward),
        (far[n.panel : 2 * n.panel, :], 2 * outward),
        (partner_far[0 : n.panel, :], -2 * outward),
        (partner_far[n.panel : 2 * n.panel, :], -3 * outward),
    ):
        total = total + pltpu.roll(table, (offset * ATOM_DEV + LANES) % LANES, 1)
    count = strength.shape[1]
    near = strength[...]
    if count < LANES:
        near = jnp.concatenate([near, jnp.zeros((1, LANES - count), jnp.float32)], axis=1)
    near = jnp.broadcast_to(near, total.shape)
    near = pltpu.roll(near, (ATOM_DEV - slab * ATOM_DEV + LANES) % LANES, 1)
    lane = lax.broadcasted_iota(jnp.int32, total.shape, 1)
    return jnp.where(lane < 3 * ATOM_DEV, total * near, 0.0)


def on_planes(n, sums):
    wide = sums
    for plane in range(1, n.depth):
        wide = wide + pltpu.roll(sums, plane * SLOTS, 1)
    return wide[:, 0 : n.atoms]


def by_side(inner, outer, run):
    odd = lax.axis_index("grid") % 2
    pl.when(odd == 0)(functools.partial(run, outer, inner))
    pl.when(odd == 1)(functools.partial(run, inner, outer))


def level_of(n, potential, plane, block, part):
    first = plane * (PLANE // LANES) + block * (BLOCK // LANES) + part * (TILE // LANES)
    return jnp.concatenate(
        [
            jnp.broadcast_to(potential[pl.ds(first + k, 1), :], (n.panel, LANES))
            for k in range(TILE // LANES)
        ],
        axis=1,
    )


def local_part(n, field, potential, sums, emit):
    for chunk in range(len(CHUNKS)):

        def one(block):
            for part in range(BLOCK // TILE):
                starts = [n.start(plane, block, part) for plane in range(n.depth)]
                planes = [field[:, pl.ds(start, TILE)].astype(jnp.float32) for start in starts]
                for plane in range(n.depth):
                    row = aligned(block * n.stride + plane * n.panel, 8)
                    lap = (
                        3.0 * stencil_weights[0] * planes[plane]
                        + stencil_weights[1]
                        * sums[pl.ds(row, n.panel), part * TILE : (part + 1) * TILE]
                        + z_sum(planes, plane, 0)
                    )
                    level = level_of(n, potential, plane, block, part)
                    value = -0.5 * lap + (level - cheb_center) * planes[plane]
                    emit(chunk, (plane, block, part), pl.ds(starts[plane], TILE), value)

        n.each_block(chunk, one)


def lap_beside(n, low, high, starts):
    below = [low[:, pl.ds(start, TILE)].astype(jnp.float32) for start in starts]
    above = [high[:, pl.ds(start, TILE)].astype(jnp.float32) for start in starts]
    return [
        z_sum(below, plane, -n.depth) + z_sum(above, plane, n.depth) for plane in range(n.depth)
    ]


def table_kernel(n, field, entry_ref, table, partial, packed, place):
    rows = n.entries // LANES

    def entry_row(first):
        return jnp.concatenate(
            [entry_ref[first * rows + k : first * rows + k + 1, :] for k in range(rows)], axis=1
        )

    row_at, lane_at = entry_row(0), entry_row(1)
    lane = lax.broadcasted_iota(jnp.int32, (BLOCK, n.entries), 0).astype(jnp.float32)
    place[...] = jnp.where(lane == lane_at, entry_row(2), 0.0).astype(jnp.bfloat16)
    chunk = 4 * n.atoms
    for first in range(0, n.blocks * n.atoms, chunk):
        row = lax.broadcasted_iota(jnp.int32, (chunk, n.entries), 0) + first
        hit = jnp.where(row.astype(jnp.float32) == row_at, 1.0, 0.0).astype(jnp.bfloat16)
        table[first : first + chunk, :] = lax.dot_general(
            hit, place[...], (((1,), (1,)), ((), ())), preferred_element_type=jnp.float32
        ).astype(jnp.bfloat16)
    pack_planes(n, field, (packed,))
    atom_partial(n, (packed,), table, partial)


def first_local_kernel(n, field, packed, potential, taps, out, sums):
    apply_taps(n, (packed,), taps, sums)

    def emit(chunk, tile, cells, value):
        out[:, cells] = value * (1.0 / cheb_half)

    local_part(n, field, potential, sums, emit)


def first_halo_kernel(n, local, inner, outer, table, strength, *refs):
    tables, out, sents = refs[:4], refs[4], refs[5:]
    wide = on_planes(n, near_sums(n, tables, strength))
    rows = jnp.where(
        block_diagonal(n.depth, n.panel, SLOTS), jnp.concatenate([wide] * n.depth, axis=0), 0.0
    )
    rows = jnp.concatenate(split(rows), axis=1)

    def run(low, high):
        for chunk in range(len(CHUNKS)):

            def one(block):
                weights = table[pl.ds(aligned(block * n.atoms, 16), n.atoms), :]
                weights = jnp.concatenate([weights, weights], axis=0)
                spread = jnp.dot(rows, weights, preferred_element_type=jnp.float32)
                for part in range(BLOCK // TILE):
                    starts = [n.start(plane, block, part) for plane in range(n.depth)]
                    laps = lap_beside(n, low, high, starts)
                    for plane in range(n.depth):
                        near = spread[
                            plane * n.panel : (plane + 1) * n.panel,
                            part * TILE : (part + 1) * TILE,
                        ]
                        cells = pl.ds(starts[plane], TILE)
                        value = local[:, cells] + (near - 0.5 * laps[plane]) * (1.0 / cheb_half)
                        out[:, cells] = value
                        cells = pl.ds(n.chunk_start(chunk, plane, block, part), TILE)
                        sents[chunk][:, cells] = value.astype(jnp.bfloat16)

            n.each_block(chunk, one)

    by_side(inner, outer, run)


def second_sums_kernel(n, field, table, partial, packed, rest):
    pack_planes(n, field, (packed, rest))
    atom_partial(n, (packed, rest), table, partial)


def second_local_kernel(n, field, initial, packed, rest, potential, taps, *refs):
    *outs, sums = refs
    apply_taps(n, (packed, rest), taps, sums)

    def emit(chunk, tile, cells, value):
        value = value * (2.0 / cheb_half) - initial[:, cells].astype(jnp.float32)
        outs[chunk][:, pl.ds(n.chunk_start(chunk, *tile), TILE)] = value

    local_part(n, field, potential, sums, emit)


def second_halo_kernel(n, chunk, local, inner, outer, out):
    def run(low, high):
        def one(block):
            for part in range(BLOCK // TILE):
                starts = [n.chunk_start(chunk, plane, block, part) for plane in range(n.depth)]
                laps = lap_beside(n, low, high, starts)
                for plane in range(n.depth):
                    cells = pl.ds(starts[plane], TILE)
                    value = local[:, cells] - laps[plane] * (1.0 / cheb_half)
                    out[:, cells] = value.astype(jnp.bfloat16)

        n.each_block(chunk, one)

    by_side(inner, outer, run)


def atoms_kernel(n, strength, *refs):
    *tables, out = refs
    out[...] = near_sums(n, tables, strength) * (2.0 / cheb_half)


def rotation_rows(n, shifts, owner, ritz):
    columns = ritz.shape[1]
    steps = ritz[...].astype(jnp.float32)
    blocks = []
    for shift in shifts:
        source = lax.axis_index("orb") + (lax.axis_size("orb") - shift)
        source = jnp.where(source >= lax.axis_size("orb"), source - lax.axis_size("orb"), source)
        total = jnp.zeros((n.panel, columns), jnp.float32)
        for step in range(ritz.shape[0] // n.panel):
            rows = steps[step * n.panel : (step + 1) * n.panel, :]
            total = total + jnp.where(owner[step] == source, rows, 0.0)
        blocks.append(total)
    weights = jnp.concatenate(blocks, axis=0)
    eye = lax.broadcasted_iota(jnp.int32, (columns, columns), 0) == lax.broadcasted_iota(
        jnp.int32, (columns, columns), 1
    )
    return lax.dot_general(
        eye.astype(jnp.float32),
        weights,
        (((1,), (1,)), ((), ())),
        precision=lax.Precision.HIGHEST,
        preferred_element_type=jnp.float32,
    )


def with_slots(rotation, added):
    both = jnp.dot(
        rotation,
        added[:, 0:SLOTS],
        precision=lax.Precision.HIGHEST,
        preferred_element_type=jnp.float32,
    )
    return jnp.concatenate([rotation, both], axis=1)


def twice(parts, table, n, plane, block):
    atoms = table[pl.ds(aligned(block * n.atoms + plane * SLOTS, 16), SLOTS), :]
    parts = parts + [atoms.astype(jnp.float32)]
    return jnp.concatenate(parts * 2, axis=0).astype(jnp.bfloat16)


def rotate_own_kernel(
    n, orbs, owner, ritz, added, panel, table, filtered, rotated, rest, rows_ref
):
    columns = ritz.shape[1]

    @pl.when(pl.program_id(0) == 0)
    def _():
        rotation = rotation_rows(n, range(orbs), owner, ritz)
        rest[...] = rotation[:, n.panel :]
        top = with_slots(rotation[:, 0 : n.panel], added[...])
        bottom = jnp.concatenate(
            [jnp.zeros((n.panel, n.panel), jnp.float32), added[:, 0:SLOTS]], axis=1
        )
        rows_ref[...] = jnp.concatenate(split(jnp.concatenate([top, bottom], axis=0)), axis=1)

    matrix = rows_ref[...]
    for at in range(STEP_PLANES * n.blocks):
        plane, block = pl.program_id(0) * STEP_PLANES + at // n.blocks, at % n.blocks
        own = panel[:, pl.ds(n.start(plane, block), BLOCK)].astype(jnp.float32)
        both = jnp.dot(
            matrix,
            twice([own], table, n, plane, block),
            preferred_element_type=jnp.float32,
        )
        cells = slice(at * BLOCK, (at + 1) * BLOCK)
        filtered[:, cells] = (own + both[columns : columns + n.panel, :]).astype(jnp.bfloat16)
        rotated[:, pl.ds(n.start(plane, block), BLOCK)] = both[0:columns, :]


def rotate_rest_kernel(n, count, rotation, *refs):
    *refs, own, table, rotated, rows_ref = refs
    adds, panels = refs[:count], refs[count:]

    @pl.when(pl.program_id(0) == 0)
    def _():
        added = jnp.concatenate([add[...] for add in adds], axis=0)
        rows_ref[...] = jnp.concatenate(split(with_slots(rotation[...], added)), axis=1)

    matrix = rows_ref[...]
    for at in range(STEP_PLANES * n.blocks):
        plane, block = pl.program_id(0) * STEP_PLANES + at // n.blocks, at % n.blocks
        cells = pl.ds(n.start(plane, block), BLOCK)
        parts = [p[:, at * BLOCK : (at + 1) * BLOCK].astype(jnp.float32) for p in panels]
        total = own[:, cells] + jnp.dot(
            matrix,
            twice(parts, table, n, plane, block),
            preferred_element_type=jnp.float32,
        )
        rotated[:, at * BLOCK : (at + 1) * BLOCK] = total.astype(jnp.bfloat16)


def call(kernel, out_shape, scratch, flops, *operands):
    bytes_accessed = sum(int(np.prod(o.shape)) * o.dtype.itemsize for o in operands)
    return pl.pallas_call(
        kernel,
        out_shape=out_shape,
        in_specs=[pl.BlockSpec(memory_space=pltpu.VMEM)] * len(operands),
        out_specs=jax.tree.map(lambda _: pl.BlockSpec(memory_space=pltpu.VMEM), out_shape),
        scratch_shapes=scratch,
        compiler_params=pltpu.CompilerParams(vmem_limit_bytes=VMEM_LIMIT),
        cost_estimate=pl.CostEstimate(
            flops=flops, bytes_accessed=bytes_accessed, transcendentals=0
        ),
    )(*operands)


def swapped(block, partner):
    count = lax.axis_size("grid")
    pairs = [(i, partner(i)) for i in range(count) if 0 <= partner(i) < count]
    return lax.ppermute(block, "grid", pairs)


def core_partner(i):
    return i ^ 1


def outer_partner(i):
    return i + 1 if i % 2 else i - 1


def exchange_sums(partial, after=None):
    partner = swapped(partial, core_partner)
    both = jnp.concatenate([partial, partner], axis=0)
    if after is not None:
        both, _ = lax.optimization_barrier((both, after))
    far = swapped(both, outer_partner)
    return partial, partner, far, swapped(far, core_partner)


def body(
    orbitals,
    potential,
    projector_atom,
    projector_cell,
    projector_value,
    atom_strength,
    ritz_rotation,
    panel_owner,
):
    panel, cells = orbitals.shape
    n = Sizes(panel, cells, projector_atom.shape[0])
    chunks = range(len(CHUNKS))
    taps = jnp.asarray(plane_taps())
    level = potential.reshape(n.cells // LANES, LANES)
    strength = atom_strength[None, :]

    bf16, f32 = jnp.bfloat16, jnp.float32
    shape = jax.ShapeDtypeStruct
    field = shape((panel, cells), f32)
    fields = [shape((panel, n.chunk_cells(chunk)), f32) for chunk in chunks]
    narrows = [shape((panel, n.chunk_cells(chunk)), bf16) for chunk in chunks]
    sums = shape((panel, LANES), f32)
    packed_shape = shape(((n.blocks + 2) * n.stride, BLOCK), bf16)
    tap_sums = pltpu.VMEM((n.blocks * n.stride, BLOCK), f32)

    outer = swapped(orbitals, outer_partner)
    inner = swapped(orbitals, core_partner)
    plane, inside = projector_cell // PLANE, projector_cell % PLANE
    slot = projector_atom - (lax.axis_index("grid") - 1) * ATOM_DEV
    row_at = ((inside // BLOCK) * n.depth + plane) * SLOTS + slot
    entries = jnp.concatenate(
        [
            entry.astype(f32).reshape(n.entries // LANES, LANES)
            for entry in (row_at, inside % BLOCK, projector_value)
        ],
        axis=0,
    )
    table, partial, packed = call(
        functools.partial(table_kernel, n),
        (shape((n.blocks * n.atoms, BLOCK), bf16), sums, packed_shape),
        [pltpu.VMEM((BLOCK, n.entries), bf16)],
        4 * 10**9,
        orbitals, entries,
    )
    local = call(
        functools.partial(first_local_kernel, n), field, [tap_sums], 2 * 10**9,
        orbitals, packed, level, taps,
    )
    near = exchange_sums(partial, local)
    step_field, *sents = call(
        functools.partial(first_halo_kernel, n),
        [field] + narrows, [], 10**9,
        local, inner, outer, table, strength, *near,
    )
    outers = [swapped(sent, outer_partner) for sent in sents]
    halos = [(swapped(sent, core_partner), outer) for sent, outer in zip(sents, outers)]
    partial, packed, rest = call(
        functools.partial(second_sums_kernel, n),
        (sums, packed_shape, packed_shape), [], 10**9,
        step_field, table,
    )
    locals_ = call(
        functools.partial(second_local_kernel, n), fields, [tap_sums], 3 * 10**9,
        step_field, orbitals, packed, rest, level, taps,
    )

    orb_count = lax.axis_size("orb")

    def all_orbs(block):
        return [block] + [
            lax.ppermute(block, "orb", [(i, (i + k) % orb_count) for i in range(orb_count)])
            for k in range(1, orb_count)
        ]

    near = exchange_sums(partial)
    held, _ = lax.optimization_barrier((locals_[0], near[2]))
    share = call(
        functools.partial(second_halo_kernel, n, 0), narrows[0], [], 10**9,
        held, *halos[0],
    )
    panels = all_orbs(share)
    added = call(functools.partial(atoms_kernel, n), sums, [], 10**6, strength, *near)
    adds = all_orbs(added)
    columns = ritz_rotation.shape[2]
    ritz = ritz_rotation.reshape(-1, columns)
    smem = pl.BlockSpec(memory_space=pltpu.SMEM)
    vmem = pl.BlockSpec(memory_space=pltpu.VMEM)
    planes_of = lambda rows: pl.BlockSpec((rows, STEP_PLANES * PLANE), lambda i: (0, i))
    params = pltpu.CompilerParams(vmem_limit_bytes=VMEM_LIMIT)
    rest = orb_count - 1
    filtered, rotated, rotation = pl.pallas_call(
        functools.partial(rotate_own_kernel, n, orb_count),
        grid=(n.depth // STEP_PLANES,),
        out_shape=(
            shape((panel, n.cells), bf16),
            shape((columns, n.cells), f32),
            shape((columns, rest * panel), f32),
        ),
        in_specs=[smem] + [vmem] * 4,
        out_specs=(planes_of(panel), vmem, vmem),
        scratch_shapes=[pltpu.VMEM((columns + panel, 2 * (panel + SLOTS)), bf16)],
        compiler_params=params,
    )(panel_owner, ritz, adds[0], share, table)
    rotated = pl.pallas_call(
        functools.partial(rotate_rest_kernel, n, rest),
        grid=(n.depth // STEP_PLANES,),
        out_shape=shape((columns, n.cells), bf16),
        in_specs=[vmem] * (1 + rest) + [planes_of(panel)] * rest + [vmem] * 2,
        out_specs=planes_of(columns),
        scratch_shapes=[pltpu.VMEM((columns, 2 * (rest * panel + SLOTS)), bf16)],
        compiler_params=params,
    )(rotation, *adds[1:], *panels[1:], rotated, table)
    return (filtered, rotated)


def solution(mesh):
    in_specs = (
        P("orb", "grid"),
        P("grid"),
        P("grid"),
        P("grid"),
        P("grid"),
        P(),
        P(None, None, "orb"),
        P(),
    )
    out_specs = (P("orb", "grid"), P("orb", "grid"))
    return jax.shard_map(body, mesh=mesh, in_specs=in_specs, out_specs=out_specs, check_vma=False)
```
